256 devices in a mesh: section: 8 (over x_hi, y), peer: 16 (over x_lo, z), shard: 2 (over core).
Axes of the slice: x: 4 (x_hi: 2, x_lo: 2; x = x_hi * 2 + x_lo), y: 4, z: 8, core: 2. Of those that a mesh axis runs over, the one named last changes fastest.
Arguments:
- forward_rows: bfloat16 [32768, 5120], P(('section', 'peer', 'shard')), may hold values from -6 to 6
- saved_rows: bfloat16 [32768, 5120], P(('section', 'peer', 'shard')), may hold values from -6 to 6
- output_grad: bfloat16 [32768, 5120], P(('section', 'peer', 'shard')), may hold values from -6 to 6
- norm_gain: bfloat16 [8, 5120], P('section'), may hold values from 0.5 to 2
- forward_counts: int32 [256, 16], P(('section', 'peer', 'shard')), may hold values from 0 to 16, as said below
- return_counts: int32 [256, 16], P(('section', 'peer', 'shard')), may hold values from 0 to 16, as said below
- matching: int32 [8, 16], P('section'), may hold values from 0 to 15, as said below
- down_weight: float32 [4096, 5120], P(('section', 'peer', 'shard')), may hold values from -0.078125 to 0.078125
- up_weight: float32 [4096, 5120], P(('section', 'peer', 'shard')), may hold values from -1 to 1
- down_moment: float32 [4096, 5120], P(('section', 'peer', 'shard')), may hold values from -60 to 60
- up_moment: float32 [4096, 5120], P(('section', 'peer', 'shard')), may hold values from -18 to 18
- down_square: float32 [4096, 5120], P(('section', 'peer', 'shard')), may hold values from 3 to 30
- up_square: float32 [4096, 5120], P(('section', 'peer', 'shard')), may hold values from 0.03 to 0.3
Outputs:
- arrived_rows: bfloat16 [65536, 5120], P(('section', 'peer', 'shard'))
- returned_grad: bfloat16 [65536, 5120], P(('section', 'peer', 'shard'))
- new_down_weight: float32 [4096, 5120], P(('section', 'peer', 'shard'))
- new_up_weight: float32 [4096, 5120], P(('section', 'peer', 'shard'))
- new_down_moment: float32 [4096, 5120], P(('section', 'peer', 'shard'))
- new_up_moment: float32 [4096, 5120], P(('section', 'peer', 'shard'))
- new_down_square: float32 [4096, 5120], P(('section', 'peer', 'shard'))
- new_up_square: float32 [4096, 5120], P(('section', 'peer', 'shard'))
The draws below stay inside these ranges and needn't reach their ends.
Inputs may be any that keep to these rules, and one draw needn't show every extreme that they name: `forward_counts`: each row sums to 128 and no entry exceeds 16. In every section one peer receives exactly 16 rows from every device of that section, so that its slots are full from every sender. `return_counts`: each row sums to 128 and no entry exceeds 16. In every section one peer of the previous section is sent exactly 16 rows by every device of that section. Each row pairs the 16 peers of a section: matching[s, p] = q exactly when matching[s, q] = p, and q differs from p.
All inputs are finite; a program needn't handle non-finite values.
Results may differ from the reference program's by a relative error of at most 0.0062.
Values may be sent and summed in bfloat16 or wider, within the bound.
A program may use at most 128 MiB of HBM per device.

```python
import math
from functools import partial
import jax
import jax.numpy as jnp
from jax import lax

D = 5120
RANK = 32
ROWS = 128
CAP = 16
TOKENS = 32768
N_SECTION = 8
N_PEER = 16
N_SHARD = 2


def route_counts(key):
    device_total = N_SECTION * N_PEER * N_SHARD
    target = jax.random.randint(jax.random.fold_in(key, 1), (N_SECTION,), 0, N_PEER, dtype=jnp.int32)
    target_dev = jnp.repeat(target, N_PEER * N_SHARD)
    weights = jax.random.randint(jax.random.fold_in(key, 2), (device_total, N_PEER), 2, 5, dtype=jnp.int32)
    peer_ids = jnp.arange(N_PEER, dtype=jnp.int32)
    is_target = peer_ids[None, :] == target_dev[:, None]
    weights = jnp.where(is_target, 0, weights).astype(jnp.int32)
    total_weight = jnp.sum(weights, axis=1, keepdims=True).astype(jnp.int32)
    remaining = ROWS - CAP
    base_share = (remaining * weights // total_weight).astype(jnp.int32)
    deficit = (remaining - jnp.sum(base_share, axis=1, keepdims=True)).astype(jnp.int32)
    position = (jnp.cumsum(1 - is_target.astype(jnp.int32), axis=1) - 1).astype(jnp.int32)
    extra_row = jnp.where(is_target, 0, (position < deficit).astype(jnp.int32))
    return jnp.where(is_target, CAP, base_share + extra_row).astype(jnp.int32)


def draw_forward_counts(key, part):
    key = jax.random.fold_in(key, 11)
    return route_counts(key)


def draw_return_counts(key, part):
    key = jax.random.fold_in(key, 12)
    return route_counts(key)


def draw_matching(key, part):
    key = jax.random.fold_in(key, 13)
    section_keys = jax.random.split(key, N_SECTION)

    def pair_up(section_key):
        order = jax.random.permutation(section_key, N_PEER).astype(jnp.int32)
        first_half = order[0::2]
        second_half = order[1::2]
        return jnp.zeros((N_PEER,), jnp.int32).at[first_half].set(second_half).at[second_half].set(first_half)
    return jax.vmap(pair_up)(section_keys).astype(jnp.int32)


def block_scale(stream_key, shape, shards, least, largest):
    def one(dim, shards_of):
        heights = jax.random.uniform(jax.random.fold_in(jax.random.fold_in(stream_key, 6), dim), (shards_of,), jnp.float32, least / len(shards), largest / len(shards))
        return jnp.repeat(jnp.exp(heights), shape[dim] // shards_of).reshape((-1,) + (1,) * (len(shape) - dim - 1))

    gain = one(*shards[0])
    for cut in shards[1:]:
        gain = gain * one(*cut)
    return gain


def normal_values(key, extent, scale, bound, cuts=(), kind=jnp.bfloat16):
    loudness = block_scale(key, extent, cuts, -0.22, 0.18) if cuts else 1.0
    entries = jax.random.normal(key, extent, jnp.float32) * scale * loudness
    return jnp.minimum(jnp.maximum(entries, -bound), bound).astype(kind)


def setup_inputs(seed: int = 0) -> dict:
    streams_of = jax.random.split(jax.random.key(seed), 14)
    forward_rows = normal_values(streams_of[0], (TOKENS, D), 1.0, 6.0, ((0, 256),))
    saved_rows = normal_values(streams_of[1], (TOKENS, D), 1.0, 6.0, ((0, 256),))
    output_grad = normal_values(streams_of[2], (TOKENS, D), 1.0, 6.0, ((0, 256),))
    norm_gain = jnp.clip(jnp.exp(math.log(2.0) - 1.3862944 * jax.random.uniform(streams_of[3], (N_SECTION, D), jnp.float32) ** block_scale(streams_of[3], (N_SECTION, D), ((0, 8),), -0.2, 0.2)), 0.5, 2.0).astype(jnp.bfloat16)
    forward_counts = draw_forward_counts(jax.random.fold_in(streams_of[13], 71), 0)
    return_counts = draw_return_counts(jax.random.fold_in(streams_of[13], 71), 0)
    matching = draw_matching(jax.random.fold_in(streams_of[13], 71), 0)
    down_weight = normal_values(streams_of[7], (N_SECTION * N_PEER * RANK, D), D ** -0.5, 0.078125, ((0, 256),), jnp.float32)
    up_weight = normal_values(streams_of[8], (N_SECTION * N_PEER * RANK, D), RANK ** -0.5, 1.0, ((0, 256),), jnp.float32)
    down_moment = normal_values(streams_of[9], (N_SECTION * N_PEER * RANK, D), 10.0, 60.0, ((0, 256),), jnp.float32)
    up_moment = normal_values(streams_of[10], (N_SECTION * N_PEER * RANK, D), 3.0, 18.0, ((0, 256),), jnp.float32)
    down_square = jnp.clip(jnp.exp(math.log(30.0) - 2.3025851 * jax.random.uniform(streams_of[11], (N_SECTION * N_PEER * RANK, D), jnp.float32) ** block_scale(streams_of[11], (N_SECTION * N_PEER * RANK, D), ((0, 256),), -0.2, 0.2)), 3.0, 30.0)
    up_square = jnp.clip(jnp.exp(math.log(0.3) - 2.3025852 * jax.random.uniform(streams_of[12], (N_SECTION * N_PEER * RANK, D), jnp.float32) ** block_scale(streams_of[12], (N_SECTION * N_PEER * RANK, D), ((0, 256),), -0.2, 0.2)), 0.03, 0.3)
    return dict(forward_rows=forward_rows, saved_rows=saved_rows, output_grad=output_grad, norm_gain=norm_gain, forward_counts=forward_counts, return_counts=return_counts, matching=matching, down_weight=down_weight, up_weight=up_weight, down_moment=down_moment, up_moment=up_moment, down_square=down_square, up_square=up_square)


beta_one = 0.9
beta_two = 0.999
learn_rate = 0.001
adam_eps = 1e-08
norm_eps = 1e-05
step_count = 20

def rms_inverse(values):
    widened = values.astype(jnp.float32)
    return 1.0 / jnp.sqrt(lax.optimization_barrier(jnp.mean(widened * widened, axis=-1, keepdims=True)) + norm_eps)

def silu_slope(pre_value):
    sigmoid = jax.nn.sigmoid(pre_value)
    return sigmoid * (1.0 + pre_value * (1.0 - sigmoid))

def adam_update(weight, moment, second, gradient):
    moment_new = beta_one * moment + (1.0 - beta_one) * gradient
    second_new = beta_two * second + (1.0 - beta_two) * gradient * gradient
    first_fix = 1.0 - beta_one ** step_count
    second_fix = 1.0 - beta_two ** step_count
    weight_new = weight - learn_rate * (moment_new / first_fix) / (jnp.sqrt(second_new / second_fix) + adam_eps)
    return (weight_new, moment_new, second_new)

def pack_slots(values, counts, capacity):
    peer_total = counts.shape[-1]
    per_peer = counts.reshape(peer_total).astype(jnp.int32)
    offsets = (jnp.cumsum(per_peer) - per_peer).astype(jnp.int32)
    slot_index = lax.broadcasted_iota(jnp.int32, (peer_total, capacity), 1)
    live_slot = slot_index < per_peer[:, None]
    source_row = jnp.where(live_slot, offsets[:, None] + slot_index, 0).astype(jnp.int32).reshape(peer_total * capacity)
    picked = jnp.take(values, source_row, axis=0)
    return jnp.where(live_slot.reshape(peer_total * capacity, 1), picked, jnp.zeros_like(picked))

def replica_step(operands):
    fwd_block, saved_block, grad_block, gain_row, down_w, up_w, down_m, up_m, down_v, up_v = operands
    gain_wide = gain_row.astype(jnp.float32)
    down_bf = down_w.astype(jnp.bfloat16)
    up_bf = up_w.astype(jnp.bfloat16)
    normed_f = (fwd_block.astype(jnp.float32) * rms_inverse(fwd_block) * gain_wide).astype(jnp.bfloat16)
    pre_f = jnp.dot(normed_f, down_bf.T, preferred_element_type=jnp.float32)
    act_f = jax.nn.silu(pre_f).astype(jnp.bfloat16)
    block_out = (fwd_block.astype(jnp.float32) + jnp.dot(act_f, up_bf, preferred_element_type=jnp.float32)).astype(jnp.bfloat16)
    saved_wide = saved_block.astype(jnp.float32)
    saved_inv = rms_inverse(saved_block)
    normed_s = (saved_wide * saved_inv * gain_wide).astype(jnp.bfloat16)
    pre_s = jnp.dot(normed_s, down_bf.T, preferred_element_type=jnp.float32)
    act_s = jax.nn.silu(pre_s).astype(jnp.bfloat16)
    grad_act = jnp.dot(grad_block, up_bf.T, preferred_element_type=jnp.float32)
    grad_pre = (grad_act * silu_slope(pre_s)).astype(jnp.bfloat16)
    grad_normed = jnp.dot(grad_pre, down_bf, preferred_element_type=jnp.float32)
    scaled = grad_normed * gain_wide
    inner = lax.optimization_barrier(jnp.sum(scaled * saved_wide, axis=-1, keepdims=True))
    grad_in = (grad_block.astype(jnp.float32) + scaled * saved_inv - saved_wide * (saved_inv * saved_inv * saved_inv) * inner / D).astype(jnp.bfloat16)
    grad_up = jnp.dot(act_s.T, grad_block, preferred_element_type=jnp.float32)
    grad_down = jnp.dot(grad_pre.T, normed_s, preferred_element_type=jnp.float32)
    new_down = adam_update(down_w, down_m, down_v, grad_down)
    new_up = adam_update(up_w, up_m, up_v, grad_up)
    return (block_out, grad_in, new_down[0], new_up[0], new_down[1], new_up[1], new_down[2], new_up[2])

def route(values, counts, direction):
    sectioned = values.reshape(N_SECTION, N_PEER * N_SHARD, ROWS, D)
    sectioned_counts = counts.reshape(N_SECTION, N_PEER * N_SHARD, N_PEER)

    def one_section(operands):
        section_rows, section_counts = operands
        packed = jax.vmap(partial(pack_slots, capacity=CAP))(section_rows, section_counts)
        packed = packed.reshape(N_PEER, N_SHARD, N_PEER, CAP, D)
        return jnp.transpose(packed, (2, 1, 0, 3, 4))
    arrived = lax.map(one_section, (sectioned, sectioned_counts))
    empty_section = jnp.zeros_like(arrived[:1])
    if direction > 0:
        shifted = jnp.concatenate([empty_section, arrived[:-1]], axis=0)
    else:
        shifted = jnp.concatenate([arrived[1:], empty_section], axis=0)
    return shifted.reshape(N_SECTION * N_PEER * N_SHARD * N_PEER * CAP, D)

def gossip_average(values, matching):
    sectioned = values.reshape(N_SECTION, N_PEER, RANK, D)
    partner = jax.vmap(partial(jnp.take, axis=0))(sectioned, matching)
    return ((sectioned + partner) * 0.5).reshape(values.shape)

def reference(forward_rows, saved_rows, output_grad, norm_gain, forward_counts, return_counts, matching, down_weight, up_weight, down_moment, up_moment, down_square, up_square):
    replicas = N_SECTION * N_PEER
    pair_rows = N_SHARD * ROWS

    def by_replica(values):
        return values.reshape(replicas, pair_rows, D)

    def by_params(values):
        return values.reshape(replicas, RANK, D)
    gain_rep = jnp.repeat(norm_gain, N_PEER, axis=0)
    results = lax.map(replica_step, (by_replica(forward_rows), by_replica(saved_rows), by_replica(output_grad), gain_rep, by_params(down_weight), by_params(up_weight), by_params(down_moment), by_params(up_moment), by_params(down_square), by_params(up_square)))
    arrived_rows = route(results[0].reshape(-1, ROWS, D), forward_counts, 1)
    returned_grad = route(results[1].reshape(-1, ROWS, D), return_counts, -1)
    finals = [gossip_average(results[index].reshape(replicas * RANK, D), matching) for index in range(2, 8)]
    return (arrived_rows, returned_grad, finals[0], finals[1], finals[2], finals[3], finals[4], finals[5])
```

```python
import functools

import jax
import jax.numpy as jnp
from jax import lax
from jax.experimental import pallas as pl
from jax.experimental.pallas import tpu as pltpu
from jax.sharding import PartitionSpec as P

MESH = pl.DeviceIdType.MESH
AXES = ("section", "peer", "shard")
LANE = 128
WIDE = 512
beta_one = 0.9
beta_two = 0.999
learn_rate = 0.001
adam_eps = 1e-08
norm_eps = 1e-05
step_count = 20
F32 = jnp.float32
BF16 = jnp.bfloat16


def dot_nt(a, b):
    return lax.dot_general(a, b, (((1,), (1,)), ((), ())), preferred_element_type=F32)


def dot_nn(a, b):
    return jnp.dot(a, b, preferred_element_type=F32)


def sigmoid(v):
    return 1.0 / (1.0 + jnp.exp(-v))


def kernel(
    sections,
    peers,
    near,
    x_hbm,
    y_hbm,
    g_hbm,
    gain_hbm,
    fcnt,
    rcnt,
    mat,
    dw_hbm,
    uw_hbm,
    dm_hbm,
    um_hbm,
    dv_hbm,
    uv_hbm,
    arrived,
    returned,
    o_dw,
    o_uw,
    o_dm,
    o_um,
    o_dv,
    o_uv,
    x_v,
    y_v,
    g_v,
    gain_v,
    st,
    wown,
    woth,
    pk_f,
    pk_b,
    ns,
    hot_f,
    hot_b,
    part_own,
    part_out,
    part_in,
    gs1,
    gr1,
    gs2,
    gr2,
    zero,
    in_sem,
    w_send,
    w_recv,
    p_send,
    p_recv,
    f_send,
    f_recv,
    b_send,
    b_recv,
    g1_send,
    g1_recv,
    g2_send,
    g2_recv,
    out_sem,
):
    s = lax.axis_index("section")
    p = lax.axis_index("peer")
    c = lax.axis_index("shard")
    rows, depth = x_v.shape
    unit = st.shape[1]
    cap = zero.shape[0]
    steps = depth // WIDE
    blocks = depth // LANE
    has_next = s < sections - 1
    has_prev = s > 0
    nxt = s + 1
    prv = s - 1

    def peer_at(k):
        z = lax.rem(lax.rem(p, near) + lax.rem(k, near), near)
        x = lax.rem(p // near + k // near, peers // near)
        return x * near + z

    state_hbm = (dw_hbm, uw_hbm, dm_hbm, um_hbm, dv_hbm, uv_hbm)
    outs = (o_dw, o_uw, o_dm, o_um, o_dv, o_uv)
    loads = [
        pltpu.make_async_copy(dw_hbm, st.at[0], in_sem.at[0]),
        pltpu.make_async_copy(uw_hbm, st.at[1], in_sem.at[1]),
        pltpu.make_async_copy(gain_hbm, gain_v, in_sem.at[2]),
        pltpu.make_async_copy(x_hbm, x_v, in_sem.at[3]),
        pltpu.make_async_copy(y_hbm, y_v, in_sem.at[4]),
        pltpu.make_async_copy(g_hbm, g_v, in_sem.at[5]),
    ] + [pltpu.make_async_copy(state_hbm[i], st.at[i], in_sem.at[4 + i]) for i in range(2, 6)]
    for load in loads:
        load.start()

    barrier = pltpu.get_barrier_semaphore()

    def greet(k, carry):
        q = peer_at(k)

        @pl.when(has_next)
        def _():
            pl.semaphore_signal(barrier, inc=1, device_id=(nxt, q, c), device_id_type=MESH)

        @pl.when(has_prev)
        def _():
            pl.semaphore_signal(barrier, inc=1, device_id=(prv, q, c), device_id_type=MESH)

        @pl.when(k > 0)
        def _():
            pl.semaphore_signal(barrier, inc=1, device_id=(s, q, c), device_id_type=MESH)

        return carry

    pl.semaphore_signal(barrier, inc=1, device_id=(s, p, 1 - c), device_id_type=MESH)
    lax.fori_loop(0, peers, greet, 0)

    zero[...] = jnp.zeros_like(zero)

    row_id = lax.broadcasted_iota(jnp.int32, (cap, rows), 0)
    col_id = lax.broadcasted_iota(jnp.int32, (cap, rows), 1)
    for cnt, hot in ((fcnt, hot_f), (rcnt, hot_b)):
        offset = jnp.int32(0)
        for q in range(peers):
            n = cnt[0, q]
            pick = (col_id == offset + row_id) & (row_id < n)
            hot[pl.ds(q * cap, cap), :] = jnp.where(pick, 1.0, 0.0).astype(BF16)
            offset = offset + n

    loads[0].wait()
    loads[1].wait()
    for i in range(2):
        for j in range(steps):
            wown[i, :, pl.ds(j * WIDE, WIDE)] = st[i, :, pl.ds(j * WIDE, WIDE)].astype(BF16)

    groups = 1 + jnp.where(has_next, 1, 0) + jnp.where(has_prev, 1, 0)
    pl.semaphore_wait(barrier, peers * groups)

    w_copy = pltpu.make_async_remote_copy(
        src_ref=wown,
        dst_ref=woth,
        send_sem=w_send,
        recv_sem=w_recv,
        device_id=(s, p, 1 - c),
        device_id_type=MESH,
    )
    w_copy.start()

    def inverse(ref):
        def body(j, acc):
            for t in range(WIDE // LANE):
                v = ref[:, pl.ds(pl.multiple_of(j * WIDE + t * LANE, LANE), LANE)].astype(F32)
                acc = acc + v * v
            return acc

        acc = lax.fori_loop(0, steps, body, jnp.zeros((rows, LANE), F32))
        return 1.0 / jnp.sqrt(jnp.sum(acc, axis=-1, keepdims=True) / depth + norm_eps)

    def cols(j):
        return pl.ds(pl.multiple_of(j * WIDE, WIDE), WIDE)

    loads[2].wait()
    loads[3].wait()
    r_f = inverse(x_v)

    def norm_f(j, carry):
        v = x_v[:, cols(j)].astype(F32) * r_f * gain_v[:, cols(j)].astype(F32)
        ns[:, cols(j)] = v.astype(BF16)
        return carry

    lax.fori_loop(0, steps, norm_f, 0)
    w_copy.wait()

    def pre_of(j, carry):
        own, oth = carry
        v = ns[:, cols(j)]
        return own + dot_nt(v, wown[0, :, cols(j)]), oth + dot_nt(v, woth[0, :, cols(j)])

    blank = jnp.zeros((rows, unit), F32)
    pre_own, pre_oth = lax.fori_loop(0, steps, pre_of, (blank, blank))
    act_own = (pre_own * sigmoid(pre_own)).astype(BF16)
    act_oth = (pre_oth * sigmoid(pre_oth)).astype(BF16)

    def out_f(j, carry):
        up = jnp.concatenate([wown[1, :, cols(j)], woth[1, :, cols(j)]], axis=0)
        act = jnp.concatenate([act_own, act_oth], axis=1)
        v = (x_v[:, cols(j)].astype(F32) + dot_nn(act, up)).astype(BF16)
        pk_f[:, cols(j)] = dot_nn(hot_f[...], v).astype(BF16)
        return carry

    lax.fori_loop(0, steps, out_f, 0)

    def route(k, pk, out, target, send, recv):
        q = peer_at(k)
        return pltpu.make_async_remote_copy(
            src_ref=pk.at[pl.ds(pl.multiple_of(q * cap, cap), cap)],
            dst_ref=out.at[pl.ds(pl.multiple_of(p * cap, cap), cap)],
            send_sem=send.at[k],
            recv_sem=recv.at[p],
            device_id=(target, q, c),
            device_id_type=MESH,
        )

    @pl.when(has_next)
    def _():
        def go(k, carry):
            route(k, pk_f, arrived, nxt, f_send, f_recv).start()
            return carry

        lax.fori_loop(0, peers, go, 0)

    loads[4].wait()
    r_s = inverse(y_v)

    def norm_s(j, carry):
        v = y_v[:, cols(j)].astype(F32) * r_s * gain_v[:, cols(j)].astype(F32)
        ns[:, cols(j)] = v.astype(BF16)
        return carry

    lax.fori_loop(0, steps, norm_s, 0)
    loads[5].wait()

    def pre_s_of(j, carry):
        a, b, d, e = carry
        v = ns[:, cols(j)]
        g = g_v[:, cols(j)]
        return (
            a + dot_nt(v, wown[0, :, cols(j)]),
            b + dot_nt(v, woth[0, :, cols(j)]),
            d + dot_nt(g, wown[1, :, cols(j)]),
            e + dot_nt(g, woth[1, :, cols(j)]),
        )

    s_own, s_oth, ga_own, ga_oth = lax.fori_loop(0, steps, pre_s_of, (blank, blank, blank, blank))

    pre_s = jnp.concatenate([s_own, s_oth], axis=1)
    grad_act = jnp.concatenate([ga_own, ga_oth], axis=1)
    sig = sigmoid(pre_s)
    act_s = (pre_s * sig).astype(BF16)
    grad_pre = (grad_act * (sig * (1.0 + pre_s * (1.0 - sig)))).astype(BF16)
    inner = jnp.sum(grad_pre.astype(F32) * pre_s, axis=-1, keepdims=True)
    pull = inner * r_s * r_s / depth

    def grads(j, carry):
        g = g_v[:, cols(j)]
        gu = lax.dot_general(act_s, g, (((0,), (0,)), ((), ())), preferred_element_type=F32)
        gd = lax.dot_general(
            grad_pre, ns[:, cols(j)], (((0,), (0,)), ((), ())), preferred_element_type=F32
        )
        part_own[0, :, cols(j)] = gd[:unit]
        part_out[0, :, cols(j)] = gd[unit:]
        part_own[1, :, cols(j)] = gu[:unit]
        part_out[1, :, cols(j)] = gu[unit:]
        return carry

    lax.fori_loop(0, steps, grads, 0)
    p_copy = pltpu.make_async_remote_copy(
        src_ref=part_out,
        dst_ref=part_in,
        send_sem=p_send,
        recv_sem=p_recv,
        device_id=(s, p, 1 - c),
        device_id_type=MESH,
    )
    p_copy.start()

    def out_b(j, carry):
        down = jnp.concatenate([wown[0, :, cols(j)], woth[0, :, cols(j)]], axis=0)
        u = dot_nn(grad_pre, down) * gain_v[:, cols(j)].astype(F32)
        y = y_v[:, cols(j)].astype(F32)
        v = (g_v[:, cols(j)].astype(F32) + u * r_s - y * pull).astype(BF16)
        pk_b[:, cols(j)] = dot_nn(hot_b[...], v).astype(BF16)
        return carry

    lax.fori_loop(0, steps, out_b, 0)

    for i in range(6, 10):
        loads[i].wait()
    p_copy.wait()

    first_fix = 1.0 - beta_one**step_count
    second_fix = 1.0 - beta_two**step_count

    def tile(a, j):
        return pl.ds(pl.multiple_of((a * blocks + j) * unit, unit), unit)

    def adam(j, carry):
        at = pl.ds(pl.multiple_of(j * LANE, LANE), LANE)
        for i in range(2):
            grad = part_own[i, :, at] + part_in[i, :, at]
            m = beta_one * st[2 + i, :, at] + (1.0 - beta_one) * grad
            v = beta_two * st[4 + i, :, at] + (1.0 - beta_two) * grad * grad
            w = st[i, :, at] - learn_rate * (m / first_fix) / (
                jnp.sqrt(v / second_fix) + adam_eps
            )
            for a, value in ((i, w), (2 + i, m), (4 + i, v)):
                st[a, :, at] = value
                gs1[tile(a, j), :] = value.astype(BF16)
        return carry

    lax.fori_loop(0, blocks, adam, 0)

    piece = gr1.shape[1]

    def slab(q):
        return pl.ds(pl.multiple_of(q * piece, piece), piece)

    def gossip(k, src, dst, send, recv):
        q = peer_at(k)
        return pltpu.make_async_remote_copy(
            src_ref=src(q),
            dst_ref=dst.at[p],
            send_sem=send.at[k],
            recv_sem=recv.at[p],
            device_id=(s, q, c),
            device_id_type=MESH,
        )

    def one(q):
        return gs1.at[slab(q)]

    def two(q):
        return gs2.at[q]

    def go_one(k, carry):
        gossip(k, one, gr1, g1_send, g1_recv).start()
        return carry

    lax.fori_loop(1, peers, go_one, 0)
    gr1[p] = gs1[slab(p), :]

    @pl.when(has_prev)
    def _():
        def go(k, carry):
            route(k, pk_b, returned, prv, b_send, b_recv).start()
            return carry

        lax.fori_loop(0, peers, go, 0)

    @pl.when(s == 0)
    def _():
        for q in range(peers):
            pltpu.make_async_copy(zero, arrived.at[pl.ds(q * cap, cap)], f_recv.at[q]).start()

    @pl.when(s == sections - 1)
    def _():
        for q in range(peers):
            pltpu.make_async_copy(zero, returned.at[pl.ds(q * cap, cap)], b_recv.at[q]).start()

    def wait_one(k, carry):
        q = peer_at(k)
        pltpu.make_async_copy(gr1.at[q], gr1.at[q], g1_recv.at[q]).wait()
        return carry

    lax.fori_loop(1, peers, wait_one, 0)

    def swap(q, carry):
        m = mat[0, q]
        gs2[q] = gr1[m]
        return carry

    lax.fori_loop(0, peers, swap, 0)

    def go_two(k, carry):
        gossip(k, two, gr2, g2_send, g2_recv).start()
        return carry

    lax.fori_loop(1, peers, go_two, 0)
    gr2[p] = gs2[p]

    def wait_two(k, carry):
        q = peer_at(k)
        pltpu.make_async_copy(gr2.at[q], gr2.at[q], g2_recv.at[q]).wait()
        return carry

    lax.fori_loop(1, peers, wait_two, 0)

    per = piece // unit

    def average(j, carry):
        at = pl.ds(pl.multiple_of(j * LANE, LANE), LANE)
        for a in range(6):
            t = a * blocks + j
            k = lax.rem(t, per)
            value = gr2[lax.div(t, per), pl.ds(pl.multiple_of(k * unit, unit), unit), :]
            st[a, :, at] = (st[a, :, at] + value.astype(F32)) * 0.5
        return carry

    lax.fori_loop(0, blocks, average, 0)
    stores = [pltpu.make_async_copy(st.at[a], outs[a], out_sem.at[a]) for a in range(6)]
    for store in stores:
        store.start()

    def finish(k, carry):
        pltpu.make_async_copy(
            arrived.at[pl.ds(k * cap, cap)], arrived.at[pl.ds(k * cap, cap)], f_recv.at[k]
        ).wait()
        pltpu.make_async_copy(
            returned.at[pl.ds(k * cap, cap)], returned.at[pl.ds(k * cap, cap)], b_recv.at[k]
        ).wait()

        @pl.when(has_next)
        def _():
            route(k, pk_f, arrived, nxt, f_send, f_recv).wait_send()

        @pl.when(has_prev)
        def _():
            route(k, pk_b, returned, prv, b_send, b_recv).wait_send()

        @pl.when(k > 0)
        def _():
            gossip(k, one, gr1, g1_send, g1_recv).wait_send()
            gossip(k, two, gr2, g2_send, g2_recv).wait_send()

        return carry

    lax.fori_loop(0, peers, finish, 0)
    for store in stores:
        store.wait()


def local(sections, peers, near, *args):
    rows, depth = args[0].shape
    unit = args[7].shape[0]
    cap = 2 * rows // peers
    slots = peers * cap
    flat = 6 * unit * depth // LANE
    any_spec = pl.BlockSpec(memory_space=pl.ANY)
    smem = pl.BlockSpec(memory_space=pltpu.SMEM)
    dma = pltpu.SemaphoreType.DMA
    return pl.pallas_call(
        functools.partial(kernel, sections, peers, near),
        out_shape=[jax.ShapeDtypeStruct((slots, depth), BF16)] * 2
        + [jax.ShapeDtypeStruct((unit, depth), F32)] * 6,
        in_specs=[any_spec] * 4 + [smem] * 3 + [any_spec] * 6,
        out_specs=[any_spec] * 8,
        scratch_shapes=[
            pltpu.VMEM((rows, depth), BF16),
            pltpu.VMEM((rows, depth), BF16),
            pltpu.VMEM((rows, depth), BF16),
            pltpu.VMEM((1, depth), BF16),
            pltpu.VMEM((6, unit, depth), F32),
            pltpu.VMEM((2, unit, depth), BF16),
            pltpu.VMEM((2, unit, depth), BF16),
            pltpu.VMEM((slots, depth), BF16),
            pltpu.VMEM((slots, depth), BF16),
            pltpu.VMEM((rows, depth), BF16),
            pltpu.VMEM((slots, rows), BF16),
            pltpu.VMEM((slots, rows), BF16),
            pltpu.VMEM((2, unit, depth), F32),
            pltpu.VMEM((2, unit, depth), F32),
            pltpu.VMEM((2, unit, depth), F32),
            pltpu.VMEM((flat, LANE), BF16),
            pltpu.VMEM((peers, flat // peers, LANE), BF16),
            pltpu.VMEM((peers, flat // peers, LANE), BF16),
            pltpu.VMEM((peers, flat // peers, LANE), BF16),
            pltpu.VMEM((cap, depth), BF16),
            dma((10,)),
            dma,
            dma,
            dma,
            dma,
            dma((peers,)),
            dma((peers,)),
            dma((peers,)),
            dma((peers,)),
            dma((peers,)),
            dma((peers,)),
            dma((peers,)),
            dma((peers,)),
            dma((6,)),
        ],
        compiler_params=pltpu.CompilerParams(
            collective_id=0, has_side_effects=True, vmem_limit_bytes=48 * 2**20
        ),
    )(*args)


def solution(mesh):
    sections, peers = mesh.shape["section"], mesh.shape["peer"]
    rows = P(AXES, None)
    by_section = P("section", None)
    return jax.shard_map(
        functools.partial(local, sections, peers, peers // 2),
        mesh=mesh,
        in_specs=(rows, rows, rows, by_section, rows, rows, by_section) + (rows,) * 6,
        out_specs=(rows,) * 8,
        check_vma=False,
    )
```

```python
import functools

import jax
import jax.numpy as jnp
from jax import lax
from jax.experimental import pallas as pl
from jax.experimental.pallas import tpu as pltpu
from jax.sharding import PartitionSpec as P

MESH = pl.DeviceIdType.MESH
AXES = ("section", "peer", "shard")
LANE = 128
WIDE = 512
CHUNKS = 4
RELAYS = 3
beta_one = 0.9
beta_two = 0.999
learn_rate = 0.001
adam_eps = 1e-08
norm_eps = 1e-05
step_count = 20
first_fix = 1.0 - beta_one**step_count
second_fix = 1.0 - beta_two**step_count
F32 = jnp.float32
BF16 = jnp.bfloat16


def dot_nt(a, b):
    return lax.dot_general(a, b, (((1,), (1,)), ((), ())), preferred_element_type=F32)


def dot_tn(a, b):
    return lax.dot_general(a, b, (((0,), (0,)), ((), ())), preferred_element_type=F32)


def dot_nn(a, b):
    return jnp.dot(a, b, preferred_element_type=F32)


def sigmoid(v):
    return 1.0 / (1.0 + jnp.exp(-v))


def stepped(weight, moment, second):
    return weight - learn_rate * (moment / first_fix) / (
        jnp.sqrt(second / second_fix) + adam_eps
    )


def arrived_all(ref, sem):
    pltpu.make_async_copy(ref, ref, sem).wait()


def kernel(
    sections,
    peers,
    near,
    x_hbm,
    y_hbm,
    g_hbm,
    gain_hbm,
    fcnt,
    rcnt,
    mat,
    dw_hbm,
    uw_hbm,
    dm_hbm,
    um_hbm,
    dv_hbm,
    uv_hbm,
    arrived,
    returned,
    o_dw,
    o_uw,
    o_dm,
    o_um,
    o_dv,
    o_uv,
    xu,
    wdn,
    y_v,
    g_v,
    gain_v,
    st,
    scaled,
    pk_f,
    pk_b,
    hot_f,
    hot_b,
    part_own,
    part_out,
    part_in,
    w1s,
    w1r,
    w2s,
    w2r,
    m1s,
    m1r,
    m2s,
    m2r,
    relay,
    zero,
    in_sem,
    w_send,
    w_recv,
    p_send,
    p_recv,
    f_send,
    f_recv,
    b_send,
    b_recv,
    q_send,
    q_recv,
    l_send,
    gw_sem,
    gm_sem,
    out_sem,
):
    s = lax.axis_index("section")
    p = lax.axis_index("peer")
    c = lax.axis_index("shard")
    rows, depth = y_v.shape
    unit = st.shape[1]
    cap = 2 * rows // peers
    steps = depth // WIDE
    blocks = depth // LANE
    part = depth // CHUNKS
    has_next = s < sections - 1
    has_prev = s > 0
    nxt = s + 1
    prv = s - 1
    half = sections // 2
    out_f_relays = jnp.where(has_next, jnp.maximum(s - (half - 1), 0), 0)
    out_b_relays = jnp.where(has_prev, jnp.maximum(half - s, 0), 0)
    in_f_relays = jnp.maximum(s - half, 0)
    in_b_relays = jnp.maximum(half - 1 - s, 0)

    px = p // near
    pz = lax.rem(p, near)

    def peer_at(k):
        j = k // 2
        h = (j + 1) // 2
        dz = (near // 2 - h) * (2 * lax.rem(j, 2) - 1)
        x = lax.rem(px + 1 - lax.rem(k, 2), 2)
        return x * near + lax.rem(pz + dz + near, near)

    others = peers - 1

    state_hbm = (dw_hbm, uw_hbm, dm_hbm, um_hbm, dv_hbm, uv_hbm)
    outs = (o_dw, o_uw, o_dm, o_um, o_dv, o_uv)
    loads = [
        pltpu.make_async_copy(dw_hbm, st.at[0], in_sem.at[0]),
        pltpu.make_async_copy(uw_hbm, st.at[1], in_sem.at[1]),
        pltpu.make_async_copy(gain_hbm, gain_v, in_sem.at[2]),
        pltpu.make_async_copy(x_hbm, xu.at[pl.ds(0, rows)], in_sem.at[3]),
        pltpu.make_async_copy(y_hbm, y_v, in_sem.at[4]),
        pltpu.make_async_copy(g_hbm, g_v, in_sem.at[5]),
    ] + [pltpu.make_async_copy(state_hbm[i], st.at[i], in_sem.at[4 + i]) for i in range(2, 6)]
    for load in loads:
        load.start()

    barrier = pltpu.get_barrier_semaphore()

    def greet(k, carry):
        q = peer_at(k)

        @pl.when(has_next)
        def _():
            pl.semaphore_signal(barrier, inc=1, device_id=(nxt, q, c), device_id_type=MESH)

        @pl.when(has_prev)
        def _():
            pl.semaphore_signal(barrier, inc=1, device_id=(prv, q, c), device_id_type=MESH)

        @pl.when(k < others)
        def _():
            pl.semaphore_signal(barrier, inc=1, device_id=(s, q, c), device_id_type=MESH)

        return carry

    pl.semaphore_signal(barrier, inc=1, device_id=(s, p, 1 - c), device_id_type=MESH)
    lax.fori_loop(0, peers, greet, 0)

    def tile(a, j):
        return pl.ds(pl.multiple_of((a * blocks + j) * unit, unit), unit)

    def lanes(j):
        return pl.ds(pl.multiple_of(j * LANE, LANE), LANE)

    loads[0].wait()
    loads[1].wait()

    def cast(j, carry):
        down = st[0, :, lanes(j)].astype(BF16)
        up = st[1, :, lanes(j)].astype(BF16)
        wdn[pl.ds(0, unit), lanes(j)] = down
        xu[pl.ds(rows, unit), lanes(j)] = up
        w1s[tile(0, j), :] = down
        w1s[tile(1, j), :] = up
        return carry

    lax.fori_loop(0, blocks, cast, 0)

    row_id = lax.broadcasted_iota(jnp.int32, (cap, rows), 0)
    col_id = lax.broadcasted_iota(jnp.int32, (cap, rows), 1)

    def slot_matrix(cnt, hot):
        offset = jnp.int32(0)
        for q in range(peers):
            n = cnt[0, q]
            pick = (col_id == offset + row_id) & (row_id < n)
            hot[pl.ds(q * cap, cap), :] = jnp.where(pick, 1.0, 0.0).astype(BF16)
            offset = offset + n

    slot_matrix(fcnt, hot_f)

    groups = 1 + jnp.where(has_next, 1, 0) + jnp.where(has_prev, 1, 0)
    pl.semaphore_wait(barrier, peers * groups)

    partner = (s, p, 1 - c)
    w_copies = [
        pltpu.make_async_remote_copy(
            src_ref=wdn.at[pl.ds(0, unit)],
            dst_ref=wdn.at[pl.ds(unit, unit)],
            send_sem=w_send.at[0],
            recv_sem=w_recv.at[0],
            device_id=partner,
            device_id_type=MESH,
        ),
        pltpu.make_async_remote_copy(
            src_ref=xu.at[pl.ds(rows, unit)],
            dst_ref=xu.at[pl.ds(rows + unit, unit)],
            send_sem=w_send.at[1],
            recv_sem=w_recv.at[1],
            device_id=partner,
            device_id_type=MESH,
        ),
    ]
    for copy in w_copies:
        copy.start()

    def gossip(q, src, dst, sem, which):
        return pltpu.make_async_remote_copy(
            src_ref=src,
            dst_ref=dst.at[p],
            send_sem=sem.at[2 * which],
            recv_sem=sem.at[2 * which + 1],
            device_id=(s, q, c),
            device_id_type=MESH,
        )

    def spread(src, dst, sem):
        size = dst.shape[1]

        def go(k, carry):
            q = peer_at(k)
            piece = src.at[pl.ds(pl.multiple_of(q * size, size), size)]
            gossip(q, piece, dst, sem, 0).start()
            return carry

        lax.fori_loop(0, others, go, 0)
        dst[p] = src[pl.ds(pl.multiple_of(p * size, size), size), :]

    def give_back(src, held, dst, sem):
        arrived_all(src.at[pl.ds(0, others)], sem.at[1])

        def swap(q, carry):
            m = mat[0, q]
            held[q] = src[m]
            return carry

        lax.fori_loop(0, peers, swap, 0)

        def go(k, carry):
            q = peer_at(k)
            gossip(q, held.at[q], dst, sem, 1).start()
            return carry

        lax.fori_loop(0, others, go, 0)
        dst[p] = held[p]

    spread(w1s, w1r, gw_sem)

    def cols(j):
        return pl.ds(pl.multiple_of(j * WIDE, WIDE), WIDE)

    def prepare(load):
        def body(j, acc):
            for t in range(WIDE // LANE):
                at = pl.ds(pl.multiple_of(j * WIDE + t * LANE, LANE), LANE)
                v = load(at).astype(F32)
                scaled[:, at] = (v * gain_v[:, at].astype(F32)).astype(BF16)
                acc = acc + v * v
            return acc

        acc = lax.fori_loop(0, steps, body, jnp.zeros((rows, LANE), F32))
        return 1.0 / jnp.sqrt(jnp.sum(acc, axis=-1, keepdims=True) / depth + norm_eps)

    loads[2].wait()
    loads[3].wait()
    r_f = prepare(lambda at: xu[pl.ds(0, rows), at])
    for copy in w_copies:
        copy.wait()
    pre_f = dot_nt(scaled[...], wdn[...]) * r_f
    act_f = (pre_f * sigmoid(pre_f)).astype(BF16)
    picked_f = dot_nn(hot_f[...], act_f).astype(BF16)
    mix_f = jnp.concatenate([hot_f[...], picked_f], axis=1)

    def chunk(h):
        return pl.ds(h * part, part)

    def route(k, h, pk, out, target, send, recv):
        q = peer_at(k)
        return pltpu.make_async_remote_copy(
            src_ref=pk.at[pl.ds(pl.multiple_of(q * cap, cap), cap), chunk(h)],
            dst_ref=out.at[pl.ds(pl.multiple_of(p * cap, cap), cap), chunk(h)],
            send_sem=send.at[h],
            recv_sem=recv.at[h],
            device_id=(target, q, c),
            device_id_type=MESH,
        )

    def handover(h, pk, target):
        return pltpu.make_async_remote_copy(
            src_ref=pk.at[:, chunk(h)],
            dst_ref=relay.at[h],
            send_sem=q_send.at[h],
            recv_sem=q_recv.at[h],
            device_id=(target, p, c),
            device_id_type=MESH,
        )

    def send_f(h):
        @pl.when(h < out_f_relays)
        def _():
            handover(min(h, RELAYS - 1), pk_f, nxt).start()

        @pl.when(has_next & (h >= out_f_relays))
        def _():
            def go(k, carry):
                route(k, h, pk_f, arrived, nxt, f_send, f_recv).start()
                return carry

            lax.fori_loop(0, peers, go, 0)

    def send_b(h):
        @pl.when(h < out_b_relays)
        def _():
            handover(min(h, RELAYS - 1), pk_b, prv).start()

        @pl.when(has_prev & (h >= out_b_relays))
        def _():
            def go(k, carry):
                route(k, h, pk_b, returned, prv, b_send, b_recv).start()
                return carry

            lax.fori_loop(0, peers, go, 0)

    def send_both(hf, hb):
        plain_f = has_next & (hf >= out_f_relays)
        plain_b = has_prev & (hb >= out_b_relays)

        def go(k, carry):
            @pl.when(plain_f)
            def _():
                route(k, hf, pk_f, arrived, nxt, f_send, f_recv).start()

            @pl.when(plain_b)
            def _():
                route(k, hb, pk_b, returned, prv, b_send, b_recv).start()

            return carry

        lax.fori_loop(0, peers, go, 0)

    for h in range(CHUNKS):
        for t in range(0, part, 256):
            at = pl.ds(h * part + t, 256)
            pk_f[:, at] = dot_nn(mix_f, xu[:, at]).astype(BF16)
        if h < 2:
            send_f(h)

    @pl.when(out_f_relays > 2)
    def _():
        handover(2, pk_f, nxt).start()

    loads[4].wait()
    loads[5].wait()
    slot_matrix(rcnt, hot_b)
    r_s = prepare(lambda at: y_v[:, at])
    pre_s = dot_nt(scaled[...], wdn[...]) * r_s
    grad_act = dot_nt(g_v[...], xu[pl.ds(rows, 2 * unit), :])
    sig = sigmoid(pre_s)
    act_s = (pre_s * sig).astype(BF16)
    grad_pre = grad_act * (sig * (1.0 + pre_s * (1.0 - sig)))
    pull = jnp.sum(grad_pre * pre_s, axis=-1, keepdims=True) * r_s * r_s / depth
    pre_r = (grad_pre * r_s).astype(BF16)

    def grads(j, carry):
        gu = dot_tn(act_s, g_v[:, cols(j)])
        gd = dot_tn(pre_r, scaled[:, cols(j)])
        part_own[0, :, cols(j)] = gd[:unit]
        part_out[0, :, cols(j)] = gd[unit:]
        part_own[1, :, cols(j)] = gu[:unit]
        part_out[1, :, cols(j)] = gu[unit:]
        return carry

    lax.fori_loop(0, steps, grads, 0)
    p_copy = pltpu.make_async_remote_copy(
        src_ref=part_out,
        dst_ref=part_in,
        send_sem=p_send,
        recv_sem=p_recv,
        device_id=partner,
        device_id_type=MESH,
    )
    p_copy.start()

    give_back(w1r, w2s, w2r, gw_sem)

    for h in range(CHUNKS):
        for t in range(0, part, 256):
            at = pl.ds(h * part + t, 256)
            u = dot_nn(pre_r, wdn[:, at]) * gain_v[:, at].astype(F32)
            v = g_v[:, at].astype(F32) + u - y_v[:, at].astype(F32) * pull
            pk_b[:, at] = dot_nn(hot_b[...], v.astype(BF16)).astype(BF16)
        if h < RELAYS:

            @pl.when(h < out_b_relays)
            def _():
                handover(h, pk_b, prv).start()

    for i in range(6, 10):
        loads[i].wait()
    p_copy.wait()

    def adam(j, carry):
        at = lanes(j)
        for i in range(2):
            grad = part_own[i, :, at] + part_in[i, :, at]
            m = beta_one * st[2 + i, :, at] + (1.0 - beta_one) * grad
            v = beta_two * st[4 + i, :, at] + (1.0 - beta_two) * grad * grad
            st[i, :, at] = stepped(st[i, :, at], m, v)
            st[2 + i, :, at] = m
            st[4 + i, :, at] = v
            m1s[tile(i, j), :] = m.astype(BF16)
            m1s[tile(2 + i, j), :] = v.astype(BF16)
        return carry

    lax.fori_loop(0, blocks, adam, 0)
    spread(m1s, m1r, gm_sem)

    send_both(2, 0)
    send_both(3, 1)

    def rest(k, carry):
        @pl.when(has_prev & (2 >= out_b_relays))
        def _():
            route(k, 2, pk_b, returned, prv, b_send, b_recv).start()

        @pl.when(has_prev)
        def _():
            route(k, 3, pk_b, returned, prv, b_send, b_recv).start()

        return carry

    lax.fori_loop(0, peers, rest, 0)

    @pl.when(s == 0)
    def _():
        zero[...] = jnp.zeros_like(zero)
        for h in range(CHUNKS):
            for q in range(peers):
                spot = arrived.at[pl.ds(q * cap, cap), chunk(h)]
                pltpu.make_async_copy(zero, spot, f_recv.at[h]).start()

    @pl.when(s == sections - 1)
    def _():
        zero[...] = jnp.zeros_like(zero)
        for h in range(CHUNKS):
            for q in range(peers):
                spot = returned.at[pl.ds(q * cap, cap), chunk(h)]
                pltpu.make_async_copy(zero, spot, b_recv.at[h]).start()

    def pass_on(h, out, recv):
        arrived_all(relay.at[h], q_recv.at[h])

        def go(k, carry):
            q = peer_at(k)
            pltpu.make_async_remote_copy(
                src_ref=relay.at[h, pl.ds(pl.multiple_of(q * cap, cap), cap)],
                dst_ref=out.at[pl.ds(pl.multiple_of(p * cap, cap), cap), chunk(h)],
                send_sem=l_send.at[h],
                recv_sem=recv.at[h],
                device_id=(s, q, c),
                device_id_type=MESH,
            ).start()
            return carry

        lax.fori_loop(0, others, go, 0)
        mine = pl.ds(pl.multiple_of(p * cap, cap), cap)
        pltpu.make_async_copy(relay.at[h, mine], out.at[mine, chunk(h)], recv.at[h]).start()

    for h in range(RELAYS):

        @pl.when(h < in_f_relays)
        def _():
            pass_on(h, arrived, f_recv)

        @pl.when(h < in_b_relays)
        def _():
            pass_on(h, returned, b_recv)

    give_back(m1r, m2s, m2r, gm_sem)

    arrived_all(w2r.at[pl.ds(0, others)], gw_sem.at[3])
    arrived_all(m2r.at[pl.ds(0, others)], gm_sem.at[3])

    def landed(ref, a, j):
        per = ref.shape[1] // unit
        t = a * blocks + j
        row = pl.multiple_of(lax.rem(t, per) * unit, unit)
        return ref[lax.div(t, per), pl.ds(row, unit), :].astype(F32)

    def average(j, carry):
        at = lanes(j)
        for i in range(2):
            m = landed(m2r, i, j)
            v = landed(m2r, 2 + i, j)
            w = stepped(landed(w2r, i, j), m, v)
            st[i, :, at] = (st[i, :, at] + w) * 0.5
            st[2 + i, :, at] = (st[2 + i, :, at] + m) * 0.5
            st[4 + i, :, at] = (st[4 + i, :, at] + v) * 0.5
        return carry

    lax.fori_loop(0, blocks, average, 0)
    stores = [pltpu.make_async_copy(st.at[a], outs[a], out_sem.at[a]) for a in range(6)]
    for store in stores:
        store.start()

    for ref, sem in ((w1r, gw_sem), (m1r, gm_sem)):
        arrived_all(ref.at[pl.ds(0, others)], sem.at[0])
        arrived_all(ref.at[pl.ds(0, others)], sem.at[2])
    for h in range(RELAYS):

        @pl.when((h < out_f_relays) | (h < out_b_relays))
        def _():
            arrived_all(relay.at[h], q_send.at[h])

        @pl.when((h < in_f_relays) | (h < in_b_relays))
        def _():
            arrived_all(relay.at[h, pl.ds(0, others * cap)], l_send.at[h])

    for h in range(CHUNKS):

        @pl.when(has_next & (h >= out_f_relays))
        def _():
            arrived_all(pk_f.at[:, chunk(h)], f_send.at[h])

        @pl.when(has_prev & (h >= out_b_relays))
        def _():
            arrived_all(pk_b.at[:, chunk(h)], b_send.at[h])

        arrived_all(arrived.at[:, chunk(h)], f_recv.at[h])
        arrived_all(returned.at[:, chunk(h)], b_recv.at[h])
    for store in stores:
        store.wait()


def settle(*refs):
    count = 8
    pieces = []
    for i in range(count):
        height = refs[i].shape[0]
        step = 32 if height > 32 else height
        for row in range(0, height, step):
            pieces.append((i, pl.ds(row, step)))
    holds = refs[2 * count : 3 * count]
    into, out = refs[3 * count :]
    reads = [
        pltpu.make_async_copy(refs[i].at[at], holds[i].at[at], into.at[n])
        for n, (i, at) in enumerate(pieces)
    ]
    writes = [
        pltpu.make_async_copy(holds[i].at[at], refs[count + i].at[at], out.at[n])
        for n, (i, at) in enumerate(pieces)
    ]
    for read in reads:
        read.start()
    for read, write in zip(reads, writes):
        read.wait()
        write.start()
    for write in writes:
        write.wait()


def local(sections, peers, near, *args):
    rows, depth = args[0].shape
    unit = args[7].shape[0]
    cap = 2 * rows // peers
    slots = peers * cap
    tiles = 2 * unit * depth // LANE
    any_spec = pl.BlockSpec(memory_space=pl.ANY)
    smem = pl.BlockSpec(memory_space=pltpu.SMEM)
    dma = pltpu.SemaphoreType.DMA
    shapes = [jax.ShapeDtypeStruct((slots, depth), BF16)] * 2 + [
        jax.ShapeDtypeStruct((unit, depth), F32)
    ] * 6

    def slabs(count):
        return pltpu.VMEM((peers, count * tiles // peers, LANE), BF16)

    results = pl.pallas_call(
        functools.partial(kernel, sections, peers, near),
        out_shape=shapes,
        in_specs=[any_spec] * 4 + [smem] * 3 + [any_spec] * 6,
        out_specs=[any_spec] * 8,
        scratch_shapes=[
            pltpu.VMEM((rows + 2 * unit, depth), BF16),
            pltpu.VMEM((2 * unit, depth), BF16),
            pltpu.VMEM((rows, depth), BF16),
            pltpu.VMEM((rows, depth), BF16),
            pltpu.VMEM((1, depth), BF16),
            pltpu.VMEM((6, unit, depth), F32),
            pltpu.VMEM((rows, depth), BF16),
            pltpu.VMEM((slots, depth), BF16),
            pltpu.VMEM((slots, depth), BF16),
            pltpu.VMEM((slots, rows), BF16),
            pltpu.VMEM((slots, rows), BF16),
            pltpu.VMEM((2, unit, depth), F32),
            pltpu.VMEM((2, unit, depth), F32),
            pltpu.VMEM((2, unit, depth), F32),
            pltpu.VMEM((tiles, LANE), BF16),
            slabs(1),
            slabs(1),
            slabs(1),
            pltpu.VMEM((2 * tiles, LANE), BF16),
            slabs(2),
            slabs(2),
            slabs(2),
            pltpu.VMEM((RELAYS, slots, depth // CHUNKS), BF16),
            pltpu.VMEM((cap, depth // CHUNKS), BF16),
            dma((10,)),
            dma((2,)),
            dma((2,)),
            dma,
            dma,
            dma((CHUNKS,)),
            dma((CHUNKS,)),
            dma((CHUNKS,)),
            dma((CHUNKS,)),
            dma((RELAYS,)),
            dma((RELAYS,)),
            dma((RELAYS,)),
            dma((4,)),
            dma((4,)),
            dma((6,)),
        ],
        compiler_params=pltpu.CompilerParams(
            collective_id=0, has_side_effects=True, vmem_limit_bytes=60 * 2**20
        ),
    )(*args)
    return pl.pallas_call(
        settle,
        out_shape=shapes,
        in_specs=[any_spec] * 8,
        out_specs=[any_spec] * 8,
        scratch_shapes=[pltpu.VMEM(shape.shape, shape.dtype) for shape in shapes]
        + [dma((2 * slots // 32 + 6,))] * 2,
        compiler_params=pltpu.CompilerParams(vmem_limit_bytes=60 * 2**20),
    )(*results)


def solution(mesh):
    sections, peers = mesh.shape["section"], mesh.shape["peer"]
    rows = P(AXES, None)
    by_section = P("section", None)
    return jax.shard_map(
        functools.partial(local, sections, peers, peers // 2),
        mesh=mesh,
        in_specs=(rows, rows, rows, by_section, rows, rows, by_section) + (rows,) * 6,
        out_specs=(rows,) * 8,
        check_vma=False,
    )
```

```python
import functools

import jax
import jax.numpy as jnp
from jax import lax
from jax.experimental import pallas as pl
from jax.experimental.pallas import tpu as pltpu
from jax.sharding import PartitionSpec as P

MESH = pl.DeviceIdType.MESH
AXES = ("section", "peer", "shard")
LANE = 128
WIDE = 512
CHUNKS = 4
SHARE = CHUNKS // 4
RELAYS = 3 * SHARE
FIRST = 2
TILE = 256
beta_one = 0.9
beta_two = 0.999
learn_rate = 0.001
adam_eps = 1e-08
norm_eps = 1e-05
step_count = 20
first_fix = 1.0 - beta_one**step_count
second_fix = 1.0 - beta_two**step_count
F32 = jnp.float32
BF16 = jnp.bfloat16


def dot_nt(a, b):
    return lax.dot_general(a, b, (((1,), (1,)), ((), ())), preferred_element_type=F32)


def dot_tn(a, b):
    return lax.dot_general(a, b, (((0,), (0,)), ((), ())), preferred_element_type=F32)


def dot_nn(a, b):
    return jnp.dot(a, b, preferred_element_type=F32)


def sigmoid(v):
    return 1.0 / (1.0 + jnp.exp(-v))


def stepped(weight, moment, second):
    return weight - learn_rate * (moment / first_fix) / (
        jnp.sqrt(second / second_fix) + adam_eps
    )


def arrived_all(ref, sem):
    pltpu.make_async_copy(ref, ref, sem).wait()


def kernel(
    sections,
    peers,
    near,
    x_hbm,
    y_hbm,
    g_hbm,
    gain_hbm,
    fcnt,
    rcnt,
    mat,
    dw_hbm,
    uw_hbm,
    dm_hbm,
    um_hbm,
    dv_hbm,
    uv_hbm,
    arrived,
    returned,
    o_dw,
    o_uw,
    o_dm,
    o_um,
    o_dv,
    o_uv,
    xu,
    wdn,
    y_v,
    g_v,
    gain_v,
    st,
    scaled,
    pk_f,
    pk_b,
    hot_f,
    hot_b,
    part_own,
    part_out,
    part_in,
    w1s,
    w1r,
    w2s,
    w2r,
    m1s,
    m1r,
    m2s,
    m2r,
    relay,
    zero,
    in_sem,
    w_send,
    w_recv,
    p_send,
    p_recv,
    f_send,
    f_recv,
    b_send,
    b_recv,
    q_send,
    q_recv,
    l_send,
    gw_sem,
    gm_sem,
    out_sem,
):
    s = lax.axis_index("section")
    p = lax.axis_index("peer")
    c = lax.axis_index("shard")
    rows, depth = y_v.shape
    unit = st.shape[1]
    cap = 2 * rows // peers
    steps = depth // WIDE
    blocks = depth // LANE
    part = depth // CHUNKS
    has_next = s < sections - 1
    has_prev = s > 0
    nxt = s + 1
    prv = s - 1
    half = sections // 2
    out_f_relays = SHARE * jnp.where(has_next, jnp.maximum(s - (half - 1), 0), 0)
    out_b_relays = SHARE * jnp.where(has_prev, jnp.maximum(half - s, 0), 0)
    in_f_relays = SHARE * jnp.maximum(s - half, 0)
    in_b_relays = SHARE * jnp.maximum(half - 1 - s, 0)

    px = p // near
    pz = lax.rem(p, near)

    def peer_at(k):
        j = k // 2
        h = (j + 1) // 2
        dz = (near // 2 - h) * (2 * lax.rem(j, 2) - 1)
        x = lax.rem(px + 1 - lax.rem(k, 2), 2)
        return x * near + lax.rem(pz + dz + near, near)

    others = peers - 1

    state_hbm = (dw_hbm, uw_hbm, dm_hbm, um_hbm, dv_hbm, uv_hbm)
    outs = (o_dw, o_uw, o_dm, o_um, o_dv, o_uv)
    loads = [
        pltpu.make_async_copy(dw_hbm, st.at[0], in_sem.at[0]),
        pltpu.make_async_copy(uw_hbm, st.at[1], in_sem.at[1]),
        pltpu.make_async_copy(gain_hbm, gain_v, in_sem.at[2]),
        pltpu.make_async_copy(x_hbm, xu.at[pl.ds(0, rows)], in_sem.at[3]),
        pltpu.make_async_copy(y_hbm, y_v, in_sem.at[4]),
        pltpu.make_async_copy(g_hbm, g_v, in_sem.at[5]),
    ] + [pltpu.make_async_copy(state_hbm[i], st.at[i], in_sem.at[4 + i]) for i in range(2, 6)]
    for load in loads:
        load.start()

    barrier = pltpu.get_barrier_semaphore()

    def greet(k, carry):
        q = peer_at(k)

        @pl.when(has_next)
        def _():
            pl.semaphore_signal(barrier, inc=1, device_id=(nxt, q, c), device_id_type=MESH)

        @pl.when(has_prev)
        def _():
            pl.semaphore_signal(barrier, inc=1, device_id=(prv, q, c), device_id_type=MESH)

        @pl.when(k < others)
        def _():
            pl.semaphore_signal(barrier, inc=1, device_id=(s, q, c), device_id_type=MESH)

        return carry

    pl.semaphore_signal(barrier, inc=1, device_id=(s, p, 1 - c), device_id_type=MESH)
    lax.fori_loop(0, peers, greet, 0)

    def tile(a, j):
        return pl.ds(pl.multiple_of((a * blocks + j) * unit, unit), unit)

    def lanes(j):
        return pl.ds(pl.multiple_of(j * LANE, LANE), LANE)

    loads[0].wait()
    loads[1].wait()

    def cast(j, carry):
        down = st[0, :, lanes(j)].astype(BF16)
        up = st[1, :, lanes(j)].astype(BF16)
        wdn[pl.ds(0, unit), lanes(j)] = down
        xu[pl.ds(rows, unit), lanes(j)] = up
        w1s[tile(0, j), :] = down
        w1s[tile(1, j), :] = up
        return carry

    lax.fori_loop(0, blocks, cast, 0)

    row_id = lax.broadcasted_iota(jnp.int32, (cap, rows), 0)
    col_id = lax.broadcasted_iota(jnp.int32, (cap, rows), 1)

    def slot_matrix(cnt, hot):
        offset = jnp.int32(0)
        for q in range(peers):
            n = cnt[0, q]
            pick = (col_id == offset + row_id) & (row_id < n)
            hot[pl.ds(q * cap, cap), :] = jnp.where(pick, 1.0, 0.0).astype(BF16)
            offset = offset + n

    slot_matrix(fcnt, hot_f)

    groups = 1 + jnp.where(has_next, 1, 0) + jnp.where(has_prev, 1, 0)
    pl.semaphore_wait(barrier, peers * groups)

    partner = (s, p, 1 - c)
    w_copies = [
        pltpu.make_async_remote_copy(
            src_ref=wdn.at[pl.ds(0, unit)],
            dst_ref=wdn.at[pl.ds(unit, unit)],
            send_sem=w_send.at[0],
            recv_sem=w_recv.at[0],
            device_id=partner,
            device_id_type=MESH,
        ),
        pltpu.make_async_remote_copy(
            src_ref=xu.at[pl.ds(rows, unit)],
            dst_ref=xu.at[pl.ds(rows + unit, unit)],
            send_sem=w_send.at[1],
            recv_sem=w_recv.at[1],
            device_id=partner,
            device_id_type=MESH,
        ),
    ]
    for copy in w_copies:
        copy.start()

    def gossip(q, src, dst, sem, which):
        return pltpu.make_async_remote_copy(
            src_ref=src,
            dst_ref=dst.at[p],
            send_sem=sem.at[2 * which],
            recv_sem=sem.at[2 * which + 1],
            device_id=(s, q, c),
            device_id_type=MESH,
        )

    def spread(src, dst, sem):
        size = dst.shape[1]

        def go(k, carry):
            q = peer_at(k)
            piece = src.at[pl.ds(pl.multiple_of(q * size, size), size)]
            gossip(q, piece, dst, sem, 0).start()
            return carry

        lax.fori_loop(0, others, go, 0)
        dst[p] = src[pl.ds(pl.multiple_of(p * size, size), size), :]

    def give_back(src, held, dst, sem):
        arrived_all(src.at[pl.ds(0, others)], sem.at[1])

        def swap(q, carry):
            m = mat[0, q]
            held[q] = src[m]
            return carry

        lax.fori_loop(0, peers, swap, 0)

        def go(k, carry):
            q = peer_at(k)
            gossip(q, held.at[q], dst, sem, 1).start()
            return carry

        lax.fori_loop(0, others, go, 0)
        dst[p] = held[p]

    spread(w1s, w1r, gw_sem)

    def cols(j):
        return pl.ds(pl.multiple_of(j * WIDE, WIDE), WIDE)

    def inverse(load, keep):
        def body(j, acc):
            for t in range(WIDE // LANE):
                at = pl.ds(pl.multiple_of(j * WIDE + t * LANE, LANE), LANE)
                v = load(at).astype(F32)
                if keep:
                    scaled[:, at] = (v * gain_v[:, at].astype(F32)).astype(BF16)
                acc = acc + v * v
            return acc

        acc = lax.fori_loop(0, steps, body, jnp.zeros((rows, LANE), F32))
        return 1.0 / jnp.sqrt(jnp.sum(acc, axis=-1, keepdims=True) / depth + norm_eps)

    loads[2].wait()
    loads[3].wait()
    r_f = inverse(lambda at: xu[pl.ds(0, rows), at], True)
    for copy in w_copies:
        copy.wait()
    pre_f = dot_nt(scaled[...], wdn[...]) * r_f
    act_f = (pre_f * sigmoid(pre_f)).astype(BF16)
    picked_f = dot_nn(hot_f[...], act_f).astype(BF16)
    mix_f = jnp.concatenate([hot_f[...], picked_f], axis=1)

    def chunk(h):
        return pl.ds(h * part, part)

    def route(k, h, pk, out, target, send, recv):
        q = peer_at(k)
        return pltpu.make_async_remote_copy(
            src_ref=pk.at[pl.ds(pl.multiple_of(q * cap, cap), cap), chunk(h)],
            dst_ref=out.at[pl.ds(pl.multiple_of(p * cap, cap), cap), chunk(h)],
            send_sem=send.at[h],
            recv_sem=recv.at[h],
            device_id=(target, q, c),
            device_id_type=MESH,
        )

    def handover(h, pk, target):
        return pltpu.make_async_remote_copy(
            src_ref=pk.at[:, chunk(h)],
            dst_ref=relay.at[h],
            send_sem=q_send.at[h],
            recv_sem=q_recv.at[h],
            device_id=(target, p, c),
            device_id_type=MESH,
        )

    def hand_f(h):
        @pl.when(h < out_f_relays)
        def _():
            handover(h, pk_f, nxt).start()

    def hand_b(h):
        @pl.when(h < out_b_relays)
        def _():
            handover(h, pk_b, prv).start()

    def send_f(h):
        @pl.when(has_next & (h >= out_f_relays))
        def _():
            def go(k, carry):
                route(k, h, pk_f, arrived, nxt, f_send, f_recv).start()
                return carry

            lax.fori_loop(0, peers, go, 0)

    def send_b(h):
        @pl.when(has_prev & (h >= out_b_relays))
        def _():
            def go(k, carry):
                route(k, h, pk_b, returned, prv, b_send, b_recv).start()
                return carry

            lax.fori_loop(0, peers, go, 0)

    def send_both(hf, hb):
        plain_f = has_next & (hf >= out_f_relays)
        plain_b = has_prev & (hb >= out_b_relays)

        def go(k, carry):
            @pl.when(plain_f)
            def _():
                route(k, hf, pk_f, arrived, nxt, f_send, f_recv).start()

            @pl.when(plain_b)
            def _():
                route(k, hb, pk_b, returned, prv, b_send, b_recv).start()

            return carry

        lax.fori_loop(0, peers, go, 0)

    for h in range(CHUNKS):
        for t in range(0, part, TILE):
            at = pl.ds(h * part + t, TILE)
            pk_f[:, at] = dot_nn(mix_f, xu[:, at]).astype(BF16)
        if h < RELAYS:
            hand_f(h)
        if h < FIRST:
            send_f(h)

    loads[4].wait()
    loads[5].wait()
    slot_matrix(rcnt, hot_b)
    r_s = inverse(lambda at: y_v[:, at], False)

    def normed(j, carry):
        for t in range(WIDE // LANE):
            at = pl.ds(pl.multiple_of(j * WIDE + t * LANE, LANE), LANE)
            v = y_v[:, at].astype(F32) * r_s * gain_v[:, at].astype(F32)
            scaled[:, at] = v.astype(BF16)
        return carry

    lax.fori_loop(0, steps, normed, 0)
    pre_s = dot_nt(scaled[...], wdn[...])
    grad_act = dot_nt(g_v[...], xu[pl.ds(rows, 2 * unit), :])
    sig = sigmoid(pre_s)
    act_s = (pre_s * sig).astype(BF16)
    grad_pre = (grad_act * (sig * (1.0 + pre_s * (1.0 - sig)))).astype(BF16)
    pull = jnp.sum(grad_pre.astype(F32) * pre_s, axis=-1, keepdims=True) * r_s * r_s / depth

    def grads(j, carry):
        gu = dot_tn(act_s, g_v[:, cols(j)])
        gd = dot_tn(grad_pre, scaled[:, cols(j)])
        part_own[0, :, cols(j)] = gd[:unit]
        part_out[0, :, cols(j)] = gd[unit:]
        part_own[1, :, cols(j)] = gu[:unit]
        part_out[1, :, cols(j)] = gu[unit:]
        return carry

    lax.fori_loop(0, steps, grads, 0)
    p_copy = pltpu.make_async_remote_copy(
        src_ref=part_out,
        dst_ref=part_in,
        send_sem=p_send,
        recv_sem=p_recv,
        device_id=partner,
        device_id_type=MESH,
    )
    p_copy.start()

    give_back(w1r, w2s, w2r, gw_sem)

    for h in range(CHUNKS):
        for t in range(0, part, TILE):
            at = pl.ds(h * part + t, TILE)
            u = dot_nn(grad_pre, wdn[:, at]) * gain_v[:, at].astype(F32) * r_s
            v = g_v[:, at].astype(F32) + u - y_v[:, at].astype(F32) * pull
            pk_b[:, at] = dot_nn(hot_b[...], v.astype(BF16)).astype(BF16)
        if h < RELAYS:
            hand_b(h)

    for i in range(6, 10):
        loads[i].wait()
    p_copy.wait()

    def adam(j, carry):
        at = lanes(j)
        for i in range(2):
            grad = part_own[i, :, at] + part_in[i, :, at]
            m = beta_one * st[2 + i, :, at] + (1.0 - beta_one) * grad
            v = beta_two * st[4 + i, :, at] + (1.0 - beta_two) * grad * grad
            st[i, :, at] = stepped(st[i, :, at], m, v)
            st[2 + i, :, at] = m
            st[4 + i, :, at] = v
            m1s[tile(i, j), :] = m.astype(BF16)
            m1s[tile(2 + i, j), :] = v.astype(BF16)
        return carry

    lax.fori_loop(0, blocks, adam, 0)
    spread(m1s, m1r, gm_sem)

    for h in range(CHUNKS):
        if FIRST + h < CHUNKS:
            send_both(FIRST + h, h)
        else:
            send_b(h)

    @pl.when(s == 0)
    def _():
        zero[...] = jnp.zeros_like(zero)
        for h in range(CHUNKS):
            for q in range(peers):
                spot = arrived.at[pl.ds(q * cap, cap), chunk(h)]
                pltpu.make_async_copy(zero, spot, f_recv.at[h]).start()

    @pl.when(s == sections - 1)
    def _():
        zero[...] = jnp.zeros_like(zero)
        for h in range(CHUNKS):
            for q in range(peers):
                spot = returned.at[pl.ds(q * cap, cap), chunk(h)]
                pltpu.make_async_copy(zero, spot, b_recv.at[h]).start()

    def pass_on(h, out, recv):
        arrived_all(relay.at[h], q_recv.at[h])

        def go(k, carry):
            q = peer_at(k)
            pltpu.make_async_remote_copy(
                src_ref=relay.at[h, pl.ds(pl.multiple_of(q * cap, cap), cap)],
                dst_ref=out.at[pl.ds(pl.multiple_of(p * cap, cap), cap), chunk(h)],
                send_sem=l_send.at[h],
                recv_sem=recv.at[h],
                device_id=(s, q, c),
                device_id_type=MESH,
            ).start()
            return carry

        lax.fori_loop(0, others, go, 0)
        mine = pl.ds(pl.multiple_of(p * cap, cap), cap)
        pltpu.make_async_copy(relay.at[h, mine], out.at[mine, chunk(h)], recv.at[h]).start()

    give_back(m1r, m2s, m2r, gm_sem)

    for h in range(RELAYS):

        @pl.when(h < in_f_relays)
        def _():
            pass_on(h, arrived, f_recv)

        @pl.when(h < in_b_relays)
        def _():
            pass_on(h, returned, b_recv)


    arrived_all(w2r.at[pl.ds(0, others)], gw_sem.at[3])
    arrived_all(m2r.at[pl.ds(0, others)], gm_sem.at[3])

    def landed(ref, a, j):
        per = ref.shape[1] // unit
        t = a * blocks + j
        row = pl.multiple_of(lax.rem(t, per) * unit, unit)
        return ref[lax.div(t, per), pl.ds(row, unit), :].astype(F32)

    def average(j, carry):
        at = lanes(j)
        for i in range(2):
            m = landed(m2r, i, j)
            v = landed(m2r, 2 + i, j)
            w = stepped(landed(w2r, i, j), m, v)
            st[i, :, at] = (st[i, :, at] + w) * 0.5
            st[2 + i, :, at] = (st[2 + i, :, at] + m) * 0.5
            st[4 + i, :, at] = (st[4 + i, :, at] + v) * 0.5
        return carry

    lax.fori_loop(0, blocks, average, 0)
    stores = [pltpu.make_async_copy(st.at[a], outs[a], out_sem.at[a]) for a in range(6)]
    for store in stores:
        store.start()

    for ref, sem in ((w1r, gw_sem), (m1r, gm_sem)):
        arrived_all(ref.at[pl.ds(0, others)], sem.at[0])
        arrived_all(ref.at[pl.ds(0, others)], sem.at[2])
    for h in range(RELAYS):

        @pl.when((h < out_f_relays) | (h < out_b_relays))
        def _():
            arrived_all(relay.at[h], q_send.at[h])

        @pl.when((h < in_f_relays) | (h < in_b_relays))
        def _():
            arrived_all(relay.at[h, pl.ds(0, others * cap)], l_send.at[h])

    for h in range(CHUNKS):

        @pl.when(has_next & (h >= out_f_relays))
        def _():
            arrived_all(pk_f.at[:, chunk(h)], f_send.at[h])

        @pl.when(has_prev & (h >= out_b_relays))
        def _():
            arrived_all(pk_b.at[:, chunk(h)], b_send.at[h])

        arrived_all(arrived.at[:, chunk(h)], f_recv.at[h])
        arrived_all(returned.at[:, chunk(h)], b_recv.at[h])
    for store in stores:
        store.wait()


def settle(*refs):
    count = 8
    sem = refs[-1]
    copies = [pltpu.make_async_copy(refs[i], refs[count + i], sem.at[i]) for i in range(count)]
    for copy in copies:
        copy.start()
    for copy in copies:
        copy.wait()


def local(sections, peers, near, *args):
    rows, depth = args[0].shape
    unit = args[7].shape[0]
    cap = 2 * rows // peers
    slots = peers * cap
    tiles = 2 * unit * depth // LANE
    any_spec = pl.BlockSpec(memory_space=pl.ANY)
    smem = pl.BlockSpec(memory_space=pltpu.SMEM)
    dma = pltpu.SemaphoreType.DMA
    shapes = [jax.ShapeDtypeStruct((slots, depth), BF16)] * 2 + [
        jax.ShapeDtypeStruct((unit, depth), F32)
    ] * 6

    def slabs(count):
        return pltpu.VMEM((peers, count * tiles // peers, LANE), BF16)

    args = [pltpu.with_memory_space_constraint(arg, pltpu.HBM) for arg in args]
    results = pl.pallas_call(
        functools.partial(kernel, sections, peers, near),
        out_shape=[pltpu.VMEM(shape.shape, shape.dtype) for shape in shapes],
        in_specs=[any_spec] * 4 + [smem] * 3 + [any_spec] * 6,
        out_specs=[any_spec] * 8,
        scratch_shapes=[
            pltpu.VMEM((rows + 2 * unit, depth), BF16),
            pltpu.VMEM((2 * unit, depth), BF16),
            pltpu.VMEM((rows, depth), BF16),
            pltpu.VMEM((rows, depth), BF16),
            pltpu.VMEM((1, depth), BF16),
            pltpu.VMEM((6, unit, depth), F32),
            pltpu.VMEM((rows, depth), BF16),
            pltpu.VMEM((slots, depth), BF16),
            pltpu.VMEM((slots, depth), BF16),
            pltpu.VMEM((slots, rows), BF16),
            pltpu.VMEM((slots, rows), BF16),
            pltpu.VMEM((2, unit, depth), F32),
            pltpu.VMEM((2, unit, depth), F32),
            pltpu.VMEM((2, unit, depth), F32),
            pltpu.VMEM((tiles, LANE), BF16),
            slabs(1),
            slabs(1),
            slabs(1),
            pltpu.VMEM((2 * tiles, LANE), BF16),
            slabs(2),
            slabs(2),
            slabs(2),
            pltpu.VMEM((RELAYS, slots, depth // CHUNKS), BF16),
            pltpu.VMEM((cap, depth // CHUNKS), BF16),
            dma((10,)),
            dma((2,)),
            dma((2,)),
            dma,
            dma,
            dma((CHUNKS,)),
            dma((CHUNKS,)),
            dma((CHUNKS,)),
            dma((CHUNKS,)),
            dma((RELAYS,)),
            dma((RELAYS,)),
            dma((RELAYS,)),
            dma((4,)),
            dma((4,)),
            dma((6,)),
        ],
        compiler_params=pltpu.CompilerParams(
            collective_id=0, has_side_effects=True, vmem_limit_bytes=40 * 2**20
        ),
    )(*args)
    return pl.pallas_call(
        settle,
        out_shape=shapes,
        in_specs=[any_spec] * 8,
        out_specs=[any_spec] * 8,
        scratch_shapes=[dma((8,))],
        compiler_params=pltpu.CompilerParams(vmem_limit_bytes=2 * 2**20),
    )(*results)


def solution(mesh):
    sections, peers = mesh.shape["section"], mesh.shape["peer"]
    rows = P(AXES, None)
    by_section = P("section", None)
    return jax.shard_map(
        functools.partial(local, sections, peers, peers // 2),
        mesh=mesh,
        in_specs=(rows, rows, rows, by_section, rows, rows, by_section) + (rows,) * 6,
        out_specs=(rows,) * 8,
        check_vma=False,
    )
```

```python
import functools

import jax
import jax.numpy as jnp
from jax import lax
from jax.experimental import pallas as pl
from jax.experimental.pallas import tpu as pltpu
from jax.sharding import PartitionSpec as P

MESH = pl.DeviceIdType.MESH
AXES = ("section", "peer", "shard")
LANE = 128
WIDE = 512
F_SPANS = ((0, 10), (10, 10), (20, 10), (30, 10))
B_SPANS = ((0, 2), (2, 10), (12, 10), (22, 10), (32, 8))
F_RELAYS = 3
B_RELAYS = 4
FIRST = 2
GROUP = 5
beta_one = 0.9
beta_two = 0.999
learn_rate = 0.001
adam_eps = 1e-08
norm_eps = 1e-05
step_count = 20
first_fix = 1.0 - beta_one**step_count
second_fix = 1.0 - beta_two**step_count
F32 = jnp.float32
BF16 = jnp.bfloat16


def dot_nt(a, b):
    return lax.dot_general(a, b, (((1,), (1,)), ((), ())), preferred_element_type=F32)


def dot_tn(a, b):
    return lax.dot_general(a, b, (((0,), (0,)), ((), ())), preferred_element_type=F32)


def dot_nn(a, b):
    return jnp.dot(a, b, preferred_element_type=F32)


def sigmoid(v):
    return 1.0 / (1.0 + jnp.exp(-v))


def stepped(weight, moment, second):
    return weight - learn_rate * (moment / first_fix) / (
        jnp.sqrt(second / second_fix) + adam_eps
    )


def arrived_all(ref, sem):
    pltpu.make_async_copy(ref, ref, sem).wait()


def kernel(
    sections,
    peers,
    near,
    x_hbm,
    y_hbm,
    g_hbm,
    gain_hbm,
    fcnt,
    rcnt,
    mat,
    dw_hbm,
    uw_hbm,
    dm_hbm,
    um_hbm,
    dv_hbm,
    uv_hbm,
    arrived,
    returned,
    o_dw,
    o_uw,
    o_dm,
    o_um,
    o_dv,
    o_uv,
    xu,
    wdn,
    y_v,
    g_v,
    gain_v,
    st,
    scaled,
    pk_f,
    pk_b,
    hot_f,
    hot_b,
    part_own,
    part_out,
    part_in,
    w1s,
    w1r,
    w2s,
    w2r,
    m1s,
    m1r,
    m2s,
    m2r,
    relay,
    zero,
    in_sem,
    w_send,
    w_recv,
    p_send,
    p_recv,
    f_send,
    f_recv,
    b_send,
    b_recv,
    q_send,
    q_recv,
    l_send,
    gw_sem,
    gm_sem,
    out_sem,
):
    s = lax.axis_index("section")
    p = lax.axis_index("peer")
    c = lax.axis_index("shard")
    rows, depth = y_v.shape
    unit = st.shape[1]
    cap = 2 * rows // peers
    steps = depth // WIDE
    blocks = depth // LANE
    has_next = s < sections - 1
    has_prev = s > 0
    nxt = s + 1
    prv = s - 1
    half = sections // 2
    out_f_relays = jnp.where(has_next, jnp.maximum(s - (half - 1), 0), 0)
    in_f_relays = jnp.maximum(s - half, 0)
    out_b_relays = jnp.where(has_prev, jnp.maximum(half + 1 - s, 0), 0)
    in_b_relays = jnp.maximum(half - s, 0)

    px = p // near
    pz = lax.rem(p, near)

    def peer_at(k):
        j = k // 2
        h = (j + 1) // 2
        dz = (near // 2 - h) * (2 * lax.rem(j, 2) - 1)
        x = lax.rem(px + 1 - lax.rem(k, 2), 2)
        return x * near + lax.rem(pz + dz + near, near)

    others = peers - 1

    state_hbm = (dw_hbm, uw_hbm, dm_hbm, um_hbm, dv_hbm, uv_hbm)
    outs = (o_dw, o_uw, o_dm, o_um, o_dv, o_uv)
    loads = [
        pltpu.make_async_copy(dw_hbm, st.at[0], in_sem.at[0]),
        pltpu.make_async_copy(uw_hbm, st.at[1], in_sem.at[1]),
        pltpu.make_async_copy(gain_hbm, gain_v, in_sem.at[2]),
        pltpu.make_async_copy(x_hbm, xu.at[pl.ds(0, rows)], in_sem.at[3]),
        pltpu.make_async_copy(y_hbm, y_v, in_sem.at[4]),
        pltpu.make_async_copy(g_hbm, g_v, in_sem.at[5]),
    ] + [pltpu.make_async_copy(state_hbm[i], st.at[i], in_sem.at[4 + i]) for i in range(2, 6)]
    for load in loads:
        load.start()

    barrier = pltpu.get_barrier_semaphore()

    def greet(k, carry):
        q = peer_at(k)

        @pl.when(has_next)
        def _():
            pl.semaphore_signal(barrier, inc=1, device_id=(nxt, q, c), device_id_type=MESH)

        @pl.when(has_prev)
        def _():
            pl.semaphore_signal(barrier, inc=1, device_id=(prv, q, c), device_id_type=MESH)

        @pl.when(k < others)
        def _():
            pl.semaphore_signal(barrier, inc=1, device_id=(s, q, c), device_id_type=MESH)

        return carry

    pl.semaphore_signal(barrier, inc=1, device_id=(s, p, 1 - c), device_id_type=MESH)
    lax.fori_loop(0, peers, greet, 0)

    def tile(a, j):
        return pl.ds(pl.multiple_of((a * blocks + j) * unit, unit), unit)

    def lanes(j):
        return pl.ds(pl.multiple_of(j * LANE, LANE), LANE)

    loads[0].wait()
    loads[1].wait()

    def cast(n, carry):
        for t in range(GROUP):
            j = n * GROUP + t
            down = st[0, :, lanes(j)].astype(BF16)
            up = st[1, :, lanes(j)].astype(BF16)
            wdn[pl.ds(0, unit), lanes(j)] = down
            xu[pl.ds(rows, unit), lanes(j)] = up
            w1s[tile(0, j), :] = down
            w1s[tile(1, j), :] = up
        return carry

    lax.fori_loop(0, blocks // GROUP, cast, 0)

    row_id = lax.broadcasted_iota(jnp.int32, (cap, rows), 0)
    col_id = lax.broadcasted_iota(jnp.int32, (cap, rows), 1)

    def slot_matrix(cnt, hot):
        offset = jnp.int32(0)
        for q in range(peers):
            n = cnt[0, q]
            pick = (col_id == offset + row_id) & (row_id < n)
            hot[pl.ds(q * cap, cap), :] = jnp.where(pick, 1.0, 0.0).astype(BF16)
            offset = offset + n

    slot_matrix(fcnt, hot_f)

    def cols(j):
        return pl.ds(pl.multiple_of(j * WIDE, WIDE), WIDE)

    def inverse(load):
        def body(j, acc):
            for t in range(WIDE // LANE):
                v = load(pl.ds(pl.multiple_of(j * WIDE + t * LANE, LANE), LANE)).astype(F32)
                acc = acc + v * v
            return acc

        acc = lax.fori_loop(0, steps, body, jnp.zeros((rows, LANE), F32))
        return 1.0 / jnp.sqrt(jnp.sum(acc, axis=-1, keepdims=True) / depth + norm_eps)

    def normalise(load, r):
        def body(j, carry):
            for t in range(WIDE // LANE):
                at = pl.ds(pl.multiple_of(j * WIDE + t * LANE, LANE), LANE)
                v = load(at).astype(F32) * r * gain_v[:, at].astype(F32)
                scaled[:, at] = v.astype(BF16)
            return carry

        lax.fori_loop(0, steps, body, 0)

    def forward_rows(at):
        return xu[pl.ds(0, rows), at]

    groups = 1 + jnp.where(has_next, 1, 0) + jnp.where(has_prev, 1, 0)
    pl.semaphore_wait(barrier, peers * groups)

    partner = (s, p, 1 - c)
    w_copies = [
        pltpu.make_async_remote_copy(
            src_ref=wdn.at[pl.ds(0, unit)],
            dst_ref=wdn.at[pl.ds(unit, unit)],
            send_sem=w_send.at[0],
            recv_sem=w_recv.at[0],
            device_id=partner,
            device_id_type=MESH,
        ),
        pltpu.make_async_remote_copy(
            src_ref=xu.at[pl.ds(rows, unit)],
            dst_ref=xu.at[pl.ds(rows + unit, unit)],
            send_sem=w_send.at[1],
            recv_sem=w_recv.at[1],
            device_id=partner,
            device_id_type=MESH,
        ),
    ]
    for copy in w_copies:
        copy.start()

    def gossip(q, src, dst, sem, which):
        return pltpu.make_async_remote_copy(
            src_ref=src,
            dst_ref=dst.at[p],
            send_sem=sem.at[2 * which],
            recv_sem=sem.at[2 * which + 1],
            device_id=(s, q, c),
            device_id_type=MESH,
        )

    def spread(src, dst, sem):
        size = dst.shape[1]

        def go(k, carry):
            q = peer_at(k)
            piece = src.at[pl.ds(pl.multiple_of(q * size, size), size)]
            gossip(q, piece, dst, sem, 0).start()
            return carry

        lax.fori_loop(0, others, go, 0)
        dst[p] = src[pl.ds(pl.multiple_of(p * size, size), size), :]

    def give_back(src, held, dst, sem):
        arrived_all(src.at[pl.ds(0, others)], sem.at[1])

        def swap(q, carry):
            m = mat[0, q]
            held[q] = src[m]
            return carry

        lax.fori_loop(0, peers, swap, 0)

        def go(k, carry):
            q = peer_at(k)
            gossip(q, held.at[q], dst, sem, 1).start()
            return carry

        lax.fori_loop(0, others, go, 0)
        dst[p] = held[p]

    spread(w1s, w1r, gw_sem)

    loads[2].wait()
    loads[3].wait()
    normalise(forward_rows, inverse(forward_rows))
    for copy in w_copies:
        copy.wait()
    pre_f = dot_nt(scaled[...], wdn[...])
    act_f = (pre_f * sigmoid(pre_f)).astype(BF16)
    picked_f = dot_nn(hot_f[...], act_f).astype(BF16)
    mix_f = jnp.concatenate([hot_f[...], picked_f], axis=1)

    def chunk(h, spans):
        first, width = spans[h]
        return pl.ds(first * LANE, width * LANE)

    def route(k, h, pk, out, target, send, recv):
        q = peer_at(k)
        span = chunk(h, F_SPANS if pk is pk_f else B_SPANS)
        return pltpu.make_async_remote_copy(
            src_ref=pk.at[pl.ds(pl.multiple_of(q * cap, cap), cap), span],
            dst_ref=out.at[pl.ds(pl.multiple_of(p * cap, cap), cap), span],
            send_sem=send.at[h],
            recv_sem=recv.at[h],
            device_id=(target, q, c),
            device_id_type=MESH,
        )

    def handover(h, pk, target):
        span = chunk(h, F_SPANS if pk is pk_f else B_SPANS)
        return pltpu.make_async_remote_copy(
            src_ref=pk.at[:, span],
            dst_ref=relay.at[:, span],
            send_sem=q_send.at[h if pk is pk_f else len(F_SPANS) + h],
            recv_sem=q_recv.at[h],
            device_id=(target, p, c),
            device_id_type=MESH,
        )

    def hand_f(h):
        @pl.when(h < out_f_relays)
        def _():
            handover(h, pk_f, nxt).start()

    def hand_b(h):
        @pl.when(h < out_b_relays)
        def _():
            handover(h, pk_b, prv).start()

    def send_f(h):
        @pl.when(has_next & (h >= out_f_relays))
        def _():
            def go(k, carry):
                route(k, h, pk_f, arrived, nxt, f_send, f_recv).start()
                return carry

            lax.fori_loop(0, peers, go, 0)

    def send_b(h):
        @pl.when(has_prev & (h >= out_b_relays))
        def _():
            def go(k, carry):
                route(k, h, pk_b, returned, prv, b_send, b_recv).start()
                return carry

            lax.fori_loop(0, peers, go, 0)

    def send_both(hf, hb):
        plain_f = has_next & (hf >= out_f_relays)
        plain_b = has_prev & (hb >= out_b_relays)

        def go(k, carry):
            @pl.when(plain_f)
            def _():
                route(k, hf, pk_f, arrived, nxt, f_send, f_recv).start()

            @pl.when(plain_b)
            def _():
                route(k, hb, pk_b, returned, prv, b_send, b_recv).start()

            return carry

        lax.fori_loop(0, peers, go, 0)

    for h, (first, width) in enumerate(F_SPANS):
        for t in range(first, first + width, 2):
            at = pl.ds(t * LANE, 2 * LANE)
            pk_f[:, at] = dot_nn(mix_f, xu[:, at]).astype(BF16)
        if h < F_RELAYS:
            hand_f(h)
        if h < FIRST:
            send_f(h)

    loads[4].wait()
    loads[5].wait()
    slot_matrix(rcnt, hot_b)
    r_s = inverse(lambda at: y_v[:, at])
    normalise(lambda at: y_v[:, at], r_s)
    pre_s = dot_nt(scaled[...], wdn[...])
    grad_act = dot_nt(g_v[...], xu[pl.ds(rows, 2 * unit), :])
    sig = sigmoid(pre_s)
    act_s = (pre_s * sig).astype(BF16)
    grad_pre = (grad_act * (sig * (1.0 + pre_s * (1.0 - sig)))).astype(BF16)
    pull = jnp.sum(grad_pre.astype(F32) * pre_s, axis=-1, keepdims=True) * r_s * r_s / depth

    def grads(j, carry):
        gu = dot_tn(act_s, g_v[:, cols(j)])
        gd = dot_tn(grad_pre, scaled[:, cols(j)])
        part_own[0, :, cols(j)] = gd[:unit]
        part_out[0, :, cols(j)] = gd[unit:]
        part_own[1, :, cols(j)] = gu[:unit]
        part_out[1, :, cols(j)] = gu[unit:]
        return carry

    lax.fori_loop(0, steps, grads, 0)
    p_copy = pltpu.make_async_remote_copy(
        src_ref=part_out,
        dst_ref=part_in,
        send_sem=p_send,
        recv_sem=p_recv,
        device_id=partner,
        device_id_type=MESH,
    )
    p_copy.start()

    give_back(w1r, w2s, w2r, gw_sem)

    for h, (first, width) in enumerate(B_SPANS):
        for t in range(first, first + width, 2):
            at = pl.ds(t * LANE, 2 * LANE)
            u = dot_nn(grad_pre, wdn[:, at]) * gain_v[:, at].astype(F32) * r_s
            v = g_v[:, at].astype(F32) + u - y_v[:, at].astype(F32) * pull
            pk_b[:, at] = dot_nn(hot_b[...], v.astype(BF16)).astype(BF16)
        if h < B_RELAYS:
            hand_b(h)

    for i in range(6, 10):
        loads[i].wait()
    p_copy.wait()

    def adam(n, carry):
        for i, t in ((i, t) for t in range(GROUP) for i in range(2)):
            j = n * GROUP + t
            at = lanes(j)
            grad = part_own[i, :, at] + part_in[i, :, at]
            m = beta_one * st[2 + i, :, at] + (1.0 - beta_one) * grad
            v = beta_two * st[4 + i, :, at] + (1.0 - beta_two) * grad * grad
            st[i, :, at] = stepped(st[i, :, at], m, v)
            st[2 + i, :, at] = m
            st[4 + i, :, at] = v
            m1s[tile(i, j), :] = m.astype(BF16)
            m1s[tile(2 + i, j), :] = v.astype(BF16)
        return carry

    lax.fori_loop(0, blocks // GROUP, adam, 0)
    spread(m1s, m1r, gm_sem)

    for h in range(len(B_SPANS)):
        if FIRST + h < len(F_SPANS):
            send_both(FIRST + h, h)
        else:
            send_b(h)

    @pl.when(s == 0)
    def _():
        zero[...] = jnp.zeros_like(zero)
        for h, (_, width) in enumerate(F_SPANS):
            blank = zero.at[:, pl.ds(0, width * LANE)]
            for q in range(peers):
                spot = arrived.at[pl.ds(q * cap, cap), chunk(h, F_SPANS)]
                pltpu.make_async_copy(blank, spot, f_recv.at[h]).start()

    @pl.when(s == sections - 1)
    def _():
        zero[...] = jnp.zeros_like(zero)
        for h, (_, width) in enumerate(B_SPANS):
            blank = zero.at[:, pl.ds(0, width * LANE)]
            for q in range(peers):
                spot = returned.at[pl.ds(q * cap, cap), chunk(h, B_SPANS)]
                pltpu.make_async_copy(blank, spot, b_recv.at[h]).start()

    def pass_on(h, out, recv, span):
        arrived_all(relay.at[:, span], q_recv.at[h])

        def go(k, carry):
            q = peer_at(k)
            pltpu.make_async_remote_copy(
                src_ref=relay.at[pl.ds(pl.multiple_of(q * cap, cap), cap), span],
                dst_ref=out.at[pl.ds(pl.multiple_of(p * cap, cap), cap), span],
                send_sem=l_send.at[h],
                recv_sem=recv.at[h],
                device_id=(s, q, c),
                device_id_type=MESH,
            ).start()
            return carry

        lax.fori_loop(0, others, go, 0)
        mine = pl.ds(pl.multiple_of(p * cap, cap), cap)
        pltpu.make_async_copy(relay.at[mine, span], out.at[mine, span], recv.at[h]).start()

    give_back(m1r, m2s, m2r, gm_sem)

    for h in range(F_RELAYS):

        @pl.when(h < in_f_relays)
        def _():
            pass_on(h, arrived, f_recv, chunk(h, F_SPANS))

    for h in range(B_RELAYS):

        @pl.when(h < in_b_relays)
        def _():
            pass_on(h, returned, b_recv, chunk(h, B_SPANS))

    arrived_all(w2r.at[pl.ds(0, others)], gw_sem.at[3])
    arrived_all(m2r.at[pl.ds(0, others)], gm_sem.at[3])

    def landed(ref, a, j):
        per = ref.shape[1] // unit
        t = a * blocks + j
        row = pl.multiple_of(lax.rem(t, per) * unit, unit)
        return ref[lax.div(t, per), pl.ds(row, unit), :].astype(F32)

    def store(a, n):
        at = pl.ds(pl.multiple_of(n * GROUP * LANE, GROUP * LANE), GROUP * LANE)
        return pltpu.make_async_copy(st.at[a, :, at], outs[a].at[:, at], out_sem.at[a])

    def average(n, carry):
        for i, t in ((i, t) for t in range(GROUP) for i in range(2)):
            j = n * GROUP + t
            at = lanes(j)
            m = landed(m2r, i, j)
            v = landed(m2r, 2 + i, j)
            w = stepped(landed(w2r, i, j), m, v)
            st[i, :, at] = (st[i, :, at] + w) * 0.5
            st[2 + i, :, at] = (st[2 + i, :, at] + m) * 0.5
            st[4 + i, :, at] = (st[4 + i, :, at] + v) * 0.5
        for a in range(6):
            store(a, n).start()
        return carry

    lax.fori_loop(0, blocks // GROUP, average, 0)

    for ref, sem in ((w1r, gw_sem), (m1r, gm_sem)):
        arrived_all(ref.at[pl.ds(0, others)], sem.at[0])
        arrived_all(ref.at[pl.ds(0, others)], sem.at[2])
    for spans, relays, out_relays, in_relays, pk, out, send, recv, on in (
        (F_SPANS, F_RELAYS, out_f_relays, in_f_relays, pk_f, arrived, f_send, f_recv, has_next),
        (B_SPANS, B_RELAYS, out_b_relays, in_b_relays, pk_b, returned, b_send, b_recv, has_prev),
    ):
        for h in range(len(spans)):
            span = chunk(h, spans)
            if h < relays:

                @pl.when(h < out_relays)
                def _():
                    lane = h if pk is pk_f else len(F_SPANS) + h
                    arrived_all(relay.at[:, span], q_send.at[lane])

                @pl.when(h < in_relays)
                def _():
                    arrived_all(relay.at[pl.ds(0, others * cap), span], l_send.at[h])

            @pl.when(on & (h >= out_relays))
            def _():
                arrived_all(pk.at[:, span], send.at[h])

            arrived_all(out.at[:, span], recv.at[h])

    for a in range(6):
        arrived_all(st.at[a], out_sem.at[a])


def settle(*refs):
    count = 8
    sem = refs[-1]
    copies = [pltpu.make_async_copy(refs[i], refs[count + i], sem.at[i]) for i in range(count)]
    for copy in copies:
        copy.start()
    for copy in copies:
        copy.wait()


def local(sections, peers, near, *args):
    rows, depth = args[0].shape
    unit = args[7].shape[0]
    cap = 2 * rows // peers
    slots = peers * cap
    tiles = 2 * unit * depth // LANE
    any_spec = pl.BlockSpec(memory_space=pl.ANY)
    smem = pl.BlockSpec(memory_space=pltpu.SMEM)
    dma = pltpu.SemaphoreType.DMA
    shapes = [jax.ShapeDtypeStruct((slots, depth), BF16)] * 2 + [
        jax.ShapeDtypeStruct((unit, depth), F32)
    ] * 6

    def slabs(count):
        return pltpu.VMEM((peers, count * tiles // peers, LANE), BF16)

    args = [pltpu.with_memory_space_constraint(arg, pltpu.HBM) for arg in args]
    results = pl.pallas_call(
        functools.partial(kernel, sections, peers, near),
        out_shape=[pltpu.VMEM(shape.shape, shape.dtype) for shape in shapes],
        in_specs=[any_spec] * 4 + [smem] * 3 + [any_spec] * 6,
        out_specs=[any_spec] * 8,
        scratch_shapes=[
            pltpu.VMEM((rows + 2 * unit, depth), BF16),
            pltpu.VMEM((2 * unit, depth), BF16),
            pltpu.VMEM((rows, depth), BF16),
            pltpu.VMEM((rows, depth), BF16),
            pltpu.VMEM((1, depth), BF16),
            pltpu.VMEM((6, unit, depth), F32),
            pltpu.VMEM((rows, depth), BF16),
            pltpu.VMEM((slots, depth), BF16),
            pltpu.VMEM((slots, depth), BF16),
            pltpu.VMEM((slots, rows), BF16),
            pltpu.VMEM((slots, rows), BF16),
            pltpu.VMEM((2, unit, depth), F32),
            pltpu.VMEM((2, unit, depth), F32),
            pltpu.VMEM((2, unit, depth), F32),
            pltpu.VMEM((tiles, LANE), BF16),
            slabs(1),
            slabs(1),
            slabs(1),
            pltpu.VMEM((2 * tiles, LANE), BF16),
            slabs(2),
            slabs(2),
            slabs(2),
            pltpu.VMEM((slots, 32 * LANE), BF16),
            pltpu.VMEM((cap, 10 * LANE), BF16),
            dma((10,)),
            dma((2,)),
            dma((2,)),
            dma,
            dma,
            dma((4,)),
            dma((4,)),
            dma((5,)),
            dma((5,)),
            dma((8,)),
            dma((4,)),
            dma((4,)),
            dma((4,)),
            dma((4,)),
            dma((6,)),
        ],
        compiler_params=pltpu.CompilerParams(
            collective_id=0, has_side_effects=True, vmem_limit_bytes=40 * 2**20
        ),
    )(*args)
    return pl.pallas_call(
        settle,
        out_shape=shapes,
        in_specs=[any_spec] * 8,
        out_specs=[any_spec] * 8,
        scratch_shapes=[dma((8,))],
        compiler_params=pltpu.CompilerParams(vmem_limit_bytes=2 * 2**20),
    )(*results)


def solution(mesh):
    sections, peers = mesh.shape["section"], mesh.shape["peer"]
    rows = P(AXES, None)
    by_section = P("section", None)
    return jax.shard_map(
        functools.partial(local, sections, peers, peers // 2),
        mesh=mesh,
        in_specs=(rows, rows, rows, by_section, rows, rows, by_section) + (rows,) * 6,
        out_specs=(rows,) * 8,
        check_vma=False,
    )
```
